512 devices in a mesh: mesh: 8 (over x, core), fourier: 64 (over z, y).
Axes of the slice: x: 4, y: 8, z: 8, core: 2. Of those that a mesh axis runs over, the one named last changes fastest.
Arguments:
- velocity: bfloat16 [3, 2, 256, 16384], P(None, None, 'fourier', 'mesh'), may hold values from -6 to 6
- vorticity: bfloat16 [3, 2, 256, 16384], P(None, None, 'fourier', 'mesh'), may hold values from -6 to 6
- magnetic: bfloat16 [3, 2, 256, 16384], P(None, None, 'fourier', 'mesh'), may hold values from -6 to 6
- current: bfloat16 [3, 2, 256, 16384], P(None, None, 'fourier', 'mesh'), may hold values from -6 to 6
- rotation: float32 [3], replicated, may hold values from -1 to 1
- fluid_label: int32 [16384], P('mesh'), may hold values from 0 to 1, as said below
- send_rows: int32 [8, 512], P('mesh'), may hold values from 0 to 2047
- recv_rows: int32 [8, 512], P('mesh'), may hold values from 0 to 2047
Outputs:
- nonlinear_modes: bfloat16 [6, 2, 256, 16384], P(None, None, 'fourier', 'mesh')
The draws below stay inside these ranges and needn't reach their ends.
Inputs may be any that keep to these rules, and one draw needn't show every extreme that they name: `fluid_label`: each block of 2048 nodes has at most 1024 nodes with label 1, and some block has exactly 1024.
All inputs are finite; a program needn't handle non-finite values.
Results may differ from the reference program's by a relative error of at most 0.0071.
Values may be sent and summed in bfloat16 or wider, within the bound.
A program may use at most 64 MiB of HBM per device.

```python
import math
import jax
import jax.numpy as jnp
from jax import lax

MODES = 256
ANGLES = 768
NODE_BLOCK = 2048
SHARED = 512
FLUID_MAX = 1024
NODES = 16384
N_MESH = 8


def draw_fluid_label(key, part):
    block_count = NODES // NODE_BLOCK
    count_key, full_key, order_key = jax.random.split(key, 3)
    counts = jax.random.randint(count_key, (block_count,), FLUID_MAX // 4, FLUID_MAX + 1)
    full_block = jax.random.randint(full_key, (), 0, block_count)
    counts = jnp.where(jnp.arange(block_count) == full_block, FLUID_MAX, counts)
    block_keys = jax.random.split(order_key, block_count)
    ranks = jax.vmap(lambda block_key: jax.random.permutation(block_key, NODE_BLOCK))(block_keys)
    labels = (ranks < counts[:, None]).astype(jnp.int32)
    return labels.reshape(-1)


def set_ends(result, key, least, high):
    shape = result.shape
    spot = [jax.random.randint(jax.random.fold_in(key, axis), (), 0, shape[axis]) for axis in range(len(shape))]
    result = result.at[tuple(spot)].set(least)
    longest = shape.index(max(shape))
    spot[longest] = (spot[longest] + 1) % shape[longest]
    return result.at[tuple(spot)].set(high)


def block_scale(rng, extent, cuts, smallest, top_value):
    level, own = 1.0, jax.random.fold_in(rng, 6)
    for axis_at, blocks in cuts:
        heights = jnp.exp(jax.random.uniform(jax.random.fold_in(own, axis_at), (blocks,), jnp.float32, smallest / len(cuts), top_value / len(cuts)))
        level = level * jnp.repeat(heights, extent[axis_at] // blocks).reshape([-1 if axis == axis_at else 1 for axis in range(len(extent))])
    return level


def normal_values(own_key, shape, deviation, reach, cuts=(), kind=jnp.bfloat16):
    loudness = block_scale(own_key, shape, cuts, -0.22, 0.18) if cuts else 1.0
    entries = jax.random.normal(own_key, shape, jnp.float32) * deviation * loudness
    return jnp.minimum(jnp.maximum(entries, -reach), reach).astype(kind)


def setup_inputs(seed: int = 0) -> dict:
    key_of = jax.random.split(jax.random.key(seed), 9)
    velocity = normal_values(key_of[0], (3, 2, MODES, NODES), 1.0, 6.0, ((2, 64), (3, 8)))
    vorticity = normal_values(key_of[1], (3, 2, MODES, NODES), 1.0, 6.0, ((2, 64), (3, 8)))
    magnetic = normal_values(key_of[2], (3, 2, MODES, NODES), 1.0, 6.0, ((2, 64), (3, 8)))
    current = normal_values(key_of[3], (3, 2, MODES, NODES), 1.0, 6.0, ((2, 64), (3, 8)))
    rotation = jnp.clip(jax.random.uniform(key_of[4], (3,), jnp.float32, -1.0, 1.0), -1.0, 1.0)
    fluid_label = draw_fluid_label(jax.random.fold_in(key_of[8], 71), 0)
    send_rows = set_ends(jax.random.randint(key_of[6], (N_MESH, SHARED), 0, NODE_BLOCK), jax.random.fold_in(key_of[6], 1), 0, NODE_BLOCK - 1).astype(jnp.int32)
    recv_rows = set_ends(jax.random.randint(key_of[7], (N_MESH, SHARED), 0, NODE_BLOCK), jax.random.fold_in(key_of[7], 1), 0, NODE_BLOCK - 1).astype(jnp.int32)
    return {"velocity": velocity, "vorticity": vorticity, "magnetic": magnetic, "current": current, "rotation": rotation, "fluid_label": fluid_label, "send_rows": send_rows, "recv_rows": recv_rows}


def spectral_tables(mode_count, angle_count):
    mode_index = jnp.arange(mode_count, dtype=jnp.int32)
    column = jnp.arange(angle_count, dtype=jnp.int32)
    phase_index = mode_index[:, None] * column[None, :] % angle_count
    angle_grid = phase_index.astype(jnp.float32) * (2.0 * math.pi / angle_count)
    scaling = 1.0 / math.sqrt(angle_count)
    weight = jnp.where(mode_index == 0, 1.0, 2.0).astype(jnp.float32)[:, None]
    forward = jnp.stack([weight * jnp.cos(angle_grid), -weight * jnp.sin(angle_grid)]) * scaling
    inverse = jnp.stack([jnp.cos(angle_grid), -jnp.sin(angle_grid)]) * scaling
    return (forward.astype(jnp.bfloat16), inverse.astype(jnp.bfloat16))

def frame_rotation(rotation, angle_count):
    angle_grid = jnp.arange(angle_count, dtype=jnp.int32).astype(jnp.float32) * (2.0 * math.pi / angle_count)
    cosine = jnp.cos(angle_grid)
    sine_wave = jnp.sin(angle_grid)
    radial = rotation[0] * cosine + rotation[1] * sine_wave
    azimuthal = -rotation[0] * sine_wave + rotation[1] * cosine
    axial_part = jnp.zeros_like(angle_grid) + rotation[2]
    return jnp.stack([radial, azimuthal, axial_part])[:, :, None]

def cross_product(first_field, second_field):
    return jnp.stack([first_field[1] * second_field[2] - first_field[2] * second_field[1], first_field[2] * second_field[0] - first_field[0] * second_field[2], first_field[0] * second_field[1] - first_field[1] * second_field[0]])

def nonlinear(flow, vortex, bfield, jfield, frame_spin):
    force = cross_product(flow, vortex) + cross_product(jfield, bfield) - 2.0 * cross_product(frame_spin, flow)
    emotive = cross_product(flow, bfield)
    return jnp.concatenate([force, emotive], axis=0)

def reference(velocity, vorticity, magnetic, current, rotation, fluid_label, send_rows, recv_rows):
    forward, inverse = spectral_tables(MODES, ANGLES)
    forward_wide = forward.astype(jnp.float32)
    inverse_wide = inverse.astype(jnp.float32)
    frame_spin = frame_rotation(rotation, ANGLES)
    block_span = math.gcd(NODE_BLOCK, 2048)
    offsets = jnp.arange(NODES // block_span, dtype=jnp.int32) * block_span

    def one_block(offset):

        def physical(field):
            window = lax.dynamic_slice_in_dim(field, offset, block_span, 3).astype(jnp.float32)
            return jnp.einsum('crmn,rma->can', window, forward_wide, precision=lax.Precision.HIGHEST)
        fluid_mask = lax.dynamic_slice_in_dim(fluid_label, offset, block_span, 0).astype(jnp.float32)
        products = nonlinear(physical(velocity), physical(vorticity), physical(magnetic), physical(current), frame_spin)
        products = products * fluid_mask[None, None, :]
        rounded = lax.optimization_barrier(products.astype(jnp.bfloat16)).astype(jnp.float32)
        spectral = jnp.einsum('can,rma->crmn', rounded, inverse_wide, precision=lax.Precision.HIGHEST)
        return spectral.astype(jnp.bfloat16)
    pieces = lax.map(one_block, offsets)
    spectral = jnp.transpose(pieces, (1, 2, 3, 0, 4)).reshape(6, 2, MODES, NODES)
    blocks = spectral.astype(jnp.float32).reshape(6, 2, MODES, N_MESH, NODE_BLOCK)
    own_index = jnp.arange(N_MESH, dtype=jnp.int32)
    partner = jnp.bitwise_xor(own_index, 1)
    source = send_rows[partner]
    gathered = blocks[:, :, :, partner[:, None], source]
    summed = blocks.at[:, :, :, own_index[:, None], recv_rows].add(gathered)
    return summed.reshape(6, 2, MODES, NODES).astype(jnp.bfloat16)
```

```python
import functools
import math

import jax
import jax.numpy as jnp
import ml_dtypes
import numpy as np
from jax import lax
from jax.experimental import pallas as pl
from jax.experimental.pallas import tpu as pltpu
from jax.sharding import PartitionSpec as P

MESH = pl.DeviceIdType.MESH
LANES = 128
VMEM_BYTES = 62 * 1024 * 1024
def spectral_tables(modes, angles, groups):
    index = np.arange(modes, dtype=np.int64)
    phase = (index[:, None] * np.arange(angles)[None, :] % angles).astype(np.float32)
    grid = phase * np.float32(2.0 * math.pi / angles)
    scaling = np.float32(1.0 / math.sqrt(angles))
    weight = np.where(index == 0, 1.0, 2.0).astype(np.float32)[:, None]
    forward = np.stack([weight * np.cos(grid), -weight * np.sin(grid)]) * scaling
    inverse = np.stack([np.cos(grid), -np.sin(grid)]) * scaling

    def by_owner(table):
        table = table.astype(ml_dtypes.bfloat16).reshape(2, groups, modes // groups, angles)
        return table.transpose(1, 0, 2, 3).reshape(2 * modes, angles)

    return np.ascontiguousarray(by_owner(forward).T), by_owner(inverse)


def angle_tables(angles):
    grid = np.arange(angles, dtype=np.float32) * np.float32(2.0 * math.pi / angles)
    wide = lambda a: np.ascontiguousarray(np.broadcast_to(a.astype(np.float32)[:, None], (angles, LANES)))
    both = np.stack([wide(np.cos(grid)), wide(np.sin(grid))])
    both[:, :, LANES // 2 :] = 0.0
    return both


def worker_of(v, parity):
    row = v // 4
    return row * 8 + 2 * lax.rem(v, 4) + lax.rem(row + parity, 2)


def kernel(
    vel, vor, mag, cur, rot, label, send, recv, fwd, inv, trig, out,
    fields, packed, held, phys, prod, spec, own, mine, picked, given,
    fwd_v, inv_v, trig_v, rot_s, label_v, send_v, recv_v, slots, pick, chosen, place, spread,
    load_sem, small_sem, out_sem, held_sem, back_out_sem, own_sem, pair_out_sem, pair_in_sem,
):
    block = lax.axis_index("mesh")
    me = lax.axis_index("fourier")
    groups = lax.axis_size("fourier")
    half = groups // 2
    parity = lax.rem(block, 2)
    partner = block + 1 - 2 * parity
    workers = own.shape[0]
    angles = fwd_v.shape[0]
    nodes = fields.shape[4]
    tiles = nodes // LANES
    shared = send_v.shape[0] * LANES

    tile = (me // 8) * 4 + lax.rem(me, 8) // 2
    is_worker = jnp.logical_and(me < half, worker_of(tile, parity) == me)
    barrier = pltpu.get_barrier_semaphore()

    smalls = [
        pltpu.make_async_copy(label, label_v, small_sem.at[0]),
        pltpu.make_async_copy(send, send_v, small_sem.at[1]),
        pltpu.make_async_copy(recv, recv_v, small_sem.at[2]),
        pltpu.make_async_copy(rot, rot_s, small_sem.at[3]),
    ]
    loads = [
        pltpu.make_async_copy(field, fields.at[f], load_sem.at[3 + f]) for f, field in enumerate((vel, vor, mag, cur))
    ]
    tables = [
        pltpu.make_async_copy(fwd, fwd_v, load_sem.at[0]),
        pltpu.make_async_copy(inv, inv_v, load_sem.at[1]),
        pltpu.make_async_copy(trig, trig_v, load_sem.at[2]),
    ]
    for copy in smalls + loads:
        copy.start()

    @pl.when(is_worker)
    def _():
        def greet(i, _):
            pl.semaphore_signal(
                barrier, inc=1, device_id=(block, lax.rem(me + i, groups)), device_id_type=MESH
            )
            return 0

        lax.fori_loop(1, groups, greet, 0)
        for copy in tables:
            copy.start()

    pl.semaphore_signal(barrier, inc=1, device_id=(partner, me), device_id_type=MESH)

    smalls[0].wait()
    fluid = label_v[...]
    marks = fluid.astype(jnp.bfloat16)
    up_to = lax.broadcasted_iota(jnp.int32, (LANES, LANES), 0) <= lax.broadcasted_iota(jnp.int32, (LANES, LANES), 1)
    before = lax.broadcasted_iota(jnp.int32, (tiles, tiles), 1) < lax.broadcasted_iota(jnp.int32, (tiles, tiles), 0)
    f32 = jnp.float32
    inside = jnp.dot(marks, up_to.astype(f32).astype(jnp.bfloat16), preferred_element_type=f32)
    ahead = jnp.dot(before.astype(f32).astype(jnp.bfloat16), marks, preferred_element_type=f32).astype(jnp.bfloat16)
    ahead = jnp.dot(ahead, jnp.ones((LANES, LANES), jnp.bfloat16), preferred_element_type=f32)
    slot = jnp.where(fluid > 0, (inside + ahead).astype(jnp.int32) - 1, -1)
    slots[...] = slot

    for copy in loads:
        copy.wait()

    @pl.when(is_worker)
    def _():
        pl.semaphore_wait(barrier, workers)

    @pl.when(jnp.logical_not(is_worker))
    def _():
        pl.semaphore_wait(barrier, workers + 1)

    lines = fields.reshape(96, nodes)
    left = lax.broadcasted_iota(jnp.int32, (24, LANES), 1) < LANES // 2
    wide = 2 * LANES
    for q in range(spread.shape[0] // wide):
        total = jnp.zeros((96, wide), f32)
        for t in range(tiles // 2):
            at = slice(t * wide, (t + 1) * wide)
            for i in range(2):
                row = lax.broadcasted_iota(jnp.int32, (wide, LANES), 0) + q * wide
                here = slot[2 * t + i : 2 * t + i + 1, :] == row
                spread[q * wide : (q + 1) * wide, (2 * t + i) * LANES : (2 * t + i + 1) * LANES] = jnp.where(
                    here, 1.0, 0.0
                ).astype(jnp.bfloat16)
            total = total + lax.dot_general(
                lines[:, at], spread[q * wide : (q + 1) * wide, at],
                (((1,), (1,)), ((), ())), preferred_element_type=f32,
            )
        for i in range(2):
            part = total[:, i * LANES : (i + 1) * LANES]
            u, w, b, j = (part[24 * f : 24 * f + 24] for f in range(4))
            turned = [pltpu.roll(x, LANES // 2, 1) for x in (u, w, b, j)]
            first = jnp.concatenate([jnp.where(left, u, turned[3]), jnp.where(left, w, turned[2])])
            second = jnp.concatenate([jnp.where(left, turned[0], j), jnp.where(left, turned[1], b)])
            for k, slab in enumerate((first, second)):
                v = 4 * q + 2 * i + k
                packed[v] = slab.astype(jnp.bfloat16).reshape(6, 2, 4, LANES)
                owner = worker_of(jnp.int32(v), parity)

                @pl.when(owner != me)
                def _():
                    pltpu.make_async_remote_copy(
                        src_ref=packed.at[v], dst_ref=held.at[me],
                        send_sem=out_sem, recv_sem=held_sem.at[me // half],
                        device_id=(block, owner), device_id_type=MESH,
                    ).start()

                @pl.when(owner == me)
                def _():
                    pltpu.make_async_copy(packed.at[v], held.at[me], held_sem.at[me // half]).start()

    for copy in smalls[1:]:
        copy.wait()
    for r in range(shared // LANES):
        wanted = send_v[r : r + 1, :]
        here = jnp.transpose(jnp.broadcast_to(recv_v[r : r + 1, :], (LANES, LANES)))
        for v in range(tiles):
            row = lax.broadcasted_iota(jnp.int32, (LANES, LANES), 0) + v * LANES
            pick[v * LANES : (v + 1) * LANES, r * LANES : (r + 1) * LANES] = jnp.where(
                wanted == row, 1.0, 0.0
            ).astype(jnp.bfloat16)
            col = lax.broadcasted_iota(jnp.int32, (LANES, LANES), 1) + v * LANES
            place[r * LANES : (r + 1) * LANES, v * LANES : (v + 1) * LANES] = jnp.where(
                here == col, 1.0, 0.0
            ).astype(jnp.bfloat16)
    digits = jnp.zeros((8, shared), f32)
    for v in range(tiles):
        code = jnp.broadcast_to(slots[v : v + 1, :], (8, LANES)) + 32
        digit = jnp.where(lax.broadcasted_iota(jnp.int32, (8, LANES), 0) == 0, code >> 5, code & 31)
        digits = digits + jnp.dot(
            digit.astype(f32).astype(jnp.bfloat16), pick[v * LANES : (v + 1) * LANES, :], preferred_element_type=f32
        )
    code = digits.astype(jnp.int32)
    wanted = code[0:1] * 32 + code[1:2] - 32
    for s in range(spread.shape[0] // LANES):
        row = lax.broadcasted_iota(jnp.int32, (LANES, shared), 0) + s * LANES
        chosen[s * LANES : (s + 1) * LANES, :] = jnp.where(wanted == row, 1.0, 0.0).astype(jnp.bfloat16)

    @pl.when(is_worker)
    def _():
        for copy in tables:
            copy.wait()
        turn_x, turn_y, turn_z = rot_s[0] * 2.0, rot_s[1] * 2.0, rot_s[2] * 2.0
        depth = half * 8
        for h in range(2):
            arrived = held.at[pl.ds(0, half)]
            pltpu.make_async_copy(arrived, arrived, held_sem.at[h]).wait()
            for q in range(3):
                both = [
                    held[h * half : (h + 1) * half, 2 * q + i].reshape(depth, LANES) for i in range(2)
                ]
                part = jnp.dot(
                    fwd_v[:, h * depth : (h + 1) * depth],
                    jnp.concatenate(both, axis=1),
                    preferred_element_type=f32,
                )
                if h == 0:
                    phys[q] = part
                else:
                    phys[q] = phys[q] + part

        rows = 16
        near = lax.broadcasted_iota(jnp.int32, (rows, LANES), 1) < LANES // 2
        turn_z = jnp.where(near, turn_z, 0.0)

        def multiply(i, _):
            at = pl.ds(pl.multiple_of(i * rows, rows), rows)
            x = [phys[c // 2, at, (c % 2) * LANES : (c % 2 + 1) * LANES] for c in range(6)]
            cosine, sine = trig_v[0, at, :], trig_v[1, at, :]
            a, d = x[0:3], x[3:6]
            d = [d[0] + (turn_x * cosine + turn_y * sine), d[1] + (turn_y * cosine - turn_x * sine), d[2] + turn_z]
            e = [pltpu.roll(y, LANES // 2, 1) for y in a]
            for c in range(3):
                m, n = (c + 1) % 3, (c + 2) % 3
                force = a[m] * d[n] - a[n] * d[m]
                force = force + pltpu.roll(force, LANES // 2, 1)
                emf = e[m] * d[n] - e[n] * d[m]
                prod[at, c * LANES : (c + 1) * LANES] = jnp.where(near, force, emf).astype(jnp.bfloat16)
            return 0

        lax.fori_loop(0, angles // rows, multiply, 0, unroll=2)

        for h in range(2):
            back = jnp.dot(
                inv_v[h * depth : (h + 1) * depth, :], prod[...], preferred_element_type=f32
            ).astype(jnp.bfloat16)
            for c in range(3):
                spec[h * half : (h + 1) * half, c] = back[:, c * LANES : (c + 1) * LANES].reshape(half, 2, 4, LANES)

            def give(k, _):
                @pl.when(k != me)
                def _():
                    pltpu.make_async_remote_copy(
                        src_ref=spec.at[k], dst_ref=own.at[tile],
                        send_sem=back_out_sem, recv_sem=own_sem,
                        device_id=(block, k), device_id_type=MESH,
                    ).start()

                @pl.when(k == me)
                def _():
                    pltpu.make_async_copy(spec.at[k], own.at[tile], own_sem).start()

                return 0

            lax.fori_loop(h * half, (h + 1) * half, give, 0)

    pltpu.make_async_copy(own, own, own_sem).wait()
    for i in range(workers // 2):
        one, two = (own[2 * i + k].reshape(24, LANES).astype(f32) for k in range(2))
        force = jnp.where(left, one, pltpu.roll(two, LANES // 2, 1))
        emf = jnp.where(left, pltpu.roll(one, LANES // 2, 1), two)
        mine[:, i * LANES : (i + 1) * LANES] = jnp.concatenate([force, emf]).astype(jnp.bfloat16)
    picked[...] = jnp.dot(mine[...], chosen[...], preferred_element_type=f32).astype(jnp.bfloat16)
    swap = pltpu.make_async_remote_copy(
        src_ref=picked, dst_ref=given, send_sem=pair_out_sem, recv_sem=pair_in_sem,
        device_id=(partner, me), device_id_type=MESH,
    )
    swap.start()
    back = jnp.dot(mine[...], spread[...], preferred_element_type=f32)
    swap.wait_recv()
    total = back + jnp.dot(given[...], place[...], preferred_element_type=f32)
    out[...] = total.astype(jnp.bfloat16).reshape(6, 2, 4, nodes)

    swap.wait_send()

    @pl.when(is_worker)
    def _():
        sent = packed.at[pl.ds(0, workers - 1)]
        pltpu.make_async_copy(sent, sent, out_sem).wait()
        gone = spec.at[pl.ds(0, groups - 1)]
        pltpu.make_async_copy(gone, gone, back_out_sem).wait()

    @pl.when(jnp.logical_not(is_worker))
    def _():
        pltpu.make_async_copy(packed, packed, out_sem).wait()


def body(velocity, vorticity, magnetic, current, rotation, fluid_label, send_rows, recv_rows):
    groups = lax.axis_size("fourier")
    comps, parts, local, nodes = velocity.shape
    modes = groups * local
    angles = 3 * modes
    tiles = nodes // LANES
    shared = send_rows.shape[1]
    forward, inverse = spectral_tables(modes, angles, groups)
    trig = angle_tables(angles)
    half16 = jnp.bfloat16
    any_ = pl.BlockSpec(memory_space=pltpu.HBM)
    workers = 16
    fluid_most = nodes // 2
    return pl.pallas_call(
        kernel,
        out_shape=jax.ShapeDtypeStruct((2 * comps, parts, local, nodes), half16),
        in_specs=[any_] * 11,
        out_specs=pl.BlockSpec(memory_space=pltpu.VMEM),
        scratch_shapes=[
            pltpu.VMEM((4, comps, parts, local, nodes), half16),
            pltpu.VMEM((workers, 6, parts, local, LANES), half16),
            pltpu.VMEM((groups, 6, parts, local, LANES), half16),
            pltpu.VMEM((3, angles, 2 * LANES), jnp.float32),
            pltpu.VMEM((angles, 3 * LANES), half16),
            pltpu.VMEM((groups, 3, parts, local, LANES), half16),
            pltpu.VMEM((workers, 3, parts, local, LANES), half16),
            pltpu.VMEM((48, fluid_most), half16),
            pltpu.VMEM((48, shared), half16),
            pltpu.VMEM((48, shared), half16),
            pltpu.VMEM(forward.shape, half16),
            pltpu.VMEM(inverse.shape, half16),
            pltpu.VMEM(trig.shape, jnp.float32),
            pltpu.SMEM((3,), jnp.float32),
            pltpu.VMEM((tiles, LANES), jnp.int32),
            pltpu.VMEM((shared // LANES, LANES), jnp.int32),
            pltpu.VMEM((shared // LANES, LANES), jnp.int32),
            pltpu.VMEM((tiles, LANES), jnp.int32),
            pltpu.VMEM((nodes, shared), half16),
            pltpu.VMEM((fluid_most, shared), half16),
            pltpu.VMEM((shared, nodes), half16),
            pltpu.VMEM((fluid_most, nodes), half16),
            pltpu.SemaphoreType.DMA((7,)),
            pltpu.SemaphoreType.DMA((4,)),
            pltpu.SemaphoreType.DMA,
            pltpu.SemaphoreType.DMA((2,)),
            pltpu.SemaphoreType.DMA,
            pltpu.SemaphoreType.DMA,
            pltpu.SemaphoreType.DMA,
            pltpu.SemaphoreType.DMA,
        ],
        compiler_params=pltpu.CompilerParams(
            collective_id=0, has_side_effects=True, vmem_limit_bytes=VMEM_BYTES
        ),
    )(
        velocity, vorticity, magnetic, current, rotation,
        fluid_label.reshape(tiles, LANES),
        send_rows.reshape(shared // LANES, LANES),
        recv_rows.reshape(shared // LANES, LANES),
        forward, inverse, trig,
    )


def solution(mesh):
    return jax.shard_map(
        body,
        mesh=mesh,
        in_specs=(
            P(None, None, "fourier", "mesh"),
            P(None, None, "fourier", "mesh"),
            P(None, None, "fourier", "mesh"),
            P(None, None, "fourier", "mesh"),
            P(),
            P("mesh"),
            P("mesh", None),
            P("mesh", None),
        ),
        out_specs=P(None, None, "fourier", "mesh"),
        check_vma=False,
    )
```

```python
import functools
import math

import jax
import jax.numpy as jnp
import ml_dtypes
import numpy as np
from jax import lax
from jax.experimental import pallas as pl
from jax.experimental.pallas import tpu as pltpu
from jax.sharding import PartitionSpec as P

MESH = pl.DeviceIdType.MESH
LANES = 128
VMEM_BYTES = 62 * 1024 * 1024
WORKERS = (
    (0, 2, 4, 6, 9, 11, 13, 15, 16, 18, 22, 25, 31, 32, 48, 56),
    (1, 3, 5, 7, 8, 10, 12, 14, 17, 19, 21, 23, 24, 26, 30, 40),
)
def spectral_tables(modes, angles, groups):
    index = np.arange(modes, dtype=np.int64)
    phase = (index[:, None] * np.arange(angles)[None, :] % angles).astype(np.float32)
    grid = phase * np.float32(2.0 * math.pi / angles)
    scaling = np.float32(1.0 / math.sqrt(angles))
    weight = np.where(index == 0, 1.0, 2.0).astype(np.float32)[:, None]
    forward = np.stack([weight * np.cos(grid), -weight * np.sin(grid)]) * scaling
    inverse = np.stack([np.cos(grid), -np.sin(grid)]) * scaling

    def by_owner(table):
        table = table.astype(ml_dtypes.bfloat16).reshape(2, groups, modes // groups, angles)
        return table.transpose(1, 0, 2, 3).reshape(2 * modes, angles)

    return np.ascontiguousarray(by_owner(forward).T), by_owner(inverse)


def angle_tables(angles):
    grid = np.arange(angles, dtype=np.float32) * np.float32(2.0 * math.pi / angles)
    wide = lambda a: np.ascontiguousarray(np.broadcast_to(a.astype(np.float32)[:, None], (angles, LANES)))
    both = np.stack([wide(np.cos(grid)), wide(np.sin(grid))])
    both[:, :, LANES // 2 :] = 0.0
    return both


def worker_of(v, parity):
    return jnp.where(parity == 0, WORKERS[0][v], WORKERS[1][v])


def kernel(
    vel, vor, mag, cur, rot, label, send, recv, fwd, inv, trig, out,
    fields, packed, held, phys, prod, spec, own, mine, picked, given,
    fwd_v, inv_v, trig_v, rot_s, label_v, send_v, recv_v, gather, pick, chosen, place, spread,
    load_sem, small_sem, out_sem, held_sem, back_out_sem, own_sem, pair_out_sem, pair_in_sem, result, done_sem,
):
    block = lax.axis_index("mesh")
    me = lax.axis_index("fourier")
    groups = lax.axis_size("fourier")
    half = groups // 2
    parity = lax.rem(block, 2)
    partner = block + 1 - 2 * parity
    workers = own.shape[0]
    angles = fwd_v.shape[0]
    nodes = fields.shape[4]
    tiles = nodes // LANES
    shared = send_v.shape[0] * LANES

    tile = jnp.int32(0)
    works = jnp.int32(0)
    for v in range(workers):
        found = worker_of(v, parity) == me
        tile = tile + jnp.where(found, v, 0)
        works = works + jnp.where(found, 1, 0)
    is_worker = works > 0
    barrier = pltpu.get_barrier_semaphore()

    smalls = [
        pltpu.make_async_copy(label, label_v, small_sem.at[0]),
        pltpu.make_async_copy(send, send_v, small_sem.at[1]),
        pltpu.make_async_copy(recv, recv_v, small_sem.at[2]),
        pltpu.make_async_copy(rot, rot_s, small_sem.at[3]),
    ]
    loads = [
        pltpu.make_async_copy(field, fields.at[f], load_sem.at[3 + f]) for f, field in enumerate((vel, vor, mag, cur))
    ]
    tables = [
        pltpu.make_async_copy(fwd, fwd_v, load_sem.at[0]),
        pltpu.make_async_copy(inv, inv_v, load_sem.at[1]),
        pltpu.make_async_copy(trig, trig_v, load_sem.at[2]),
    ]
    for copy in smalls + loads:
        copy.start()

    @pl.when(is_worker)
    def _():
        def greet(i, _):
            pl.semaphore_signal(
                barrier, inc=1, device_id=(block, lax.rem(me + i, groups)), device_id_type=MESH
            )
            return 0

        lax.fori_loop(1, groups, greet, 0)
        for copy in tables:
            copy.start()

    pl.semaphore_signal(barrier, inc=1, device_id=(partner, me), device_id_type=MESH)

    f32 = jnp.float32
    i16 = jnp.int16
    smalls[0].wait()
    fluid = label_v[...]
    marks = fluid.astype(jnp.bfloat16)
    first = lax.broadcasted_iota(jnp.int32, (LANES, LANES), 0)
    last = lax.broadcasted_iota(jnp.int32, (LANES, LANES), 1)
    below = jnp.where(last < first, 2.0, jnp.where(last == first, 1.0, 0.0)).astype(jnp.bfloat16)
    before = lax.broadcasted_iota(jnp.int32, (tiles, tiles), 1) < lax.broadcasted_iota(jnp.int32, (tiles, tiles), 0)
    ahead = jnp.dot(before.astype(f32).astype(jnp.bfloat16), marks, preferred_element_type=f32).astype(jnp.bfloat16)
    across = (((1,), (1,)), ((), ()))
    code = lax.dot_general(below, marks, across, preferred_element_type=f32)
    code = code + lax.dot_general(
        jnp.full((LANES, LANES), 2.0, jnp.bfloat16), ahead, across, preferred_element_type=f32
    )
    code = code.astype(jnp.int32).astype(i16)

    for copy in loads:
        copy.wait()

    @pl.when(is_worker)
    def _():
        pl.semaphore_wait(barrier, workers)

    @pl.when(jnp.logical_not(is_worker))
    def _():
        pl.semaphore_wait(barrier, workers + 1)

    lines = fields.reshape(96, nodes)
    left = lax.broadcasted_iota(jnp.int32, (24, LANES), 1) < LANES // 2
    wide = 2 * LANES
    one16, zero16 = jnp.ones((LANES, LANES), jnp.bfloat16), jnp.zeros((LANES, LANES), jnp.bfloat16)
    for q in range(spread.shape[0] // wide):
        total = jnp.zeros((96, wide), f32)
        for t in range(q, tiles // 2):
            at = slice(t * wide, (t + 1) * wide)
            for n in (2 * t, 2 * t + 1):
                here = jnp.broadcast_to(code[:, n : n + 1], (LANES, LANES))
                for i in (2 * q, 2 * q + 1):
                    wanted = (last * 2 + (2 * i * LANES + 1)).astype(i16)
                    gather[n * LANES : (n + 1) * LANES, i * LANES : (i + 1) * LANES] = jnp.where(
                        here == wanted, one16, zero16
                    )
            total = total + jnp.dot(
                lines[:, at], gather[at, q * wide : (q + 1) * wide], preferred_element_type=f32
            )
        for i in range(2):
            part = total[:, i * LANES : (i + 1) * LANES]
            u, w, b, j = (part[24 * f : 24 * f + 24] for f in range(4))
            turned = [pltpu.roll(x, LANES // 2, 1) for x in (u, w, b, j)]
            slab_a = jnp.concatenate([jnp.where(left, u, turned[3]), jnp.where(left, w, turned[2])])
            slab_b = jnp.concatenate([jnp.where(left, turned[0], j), jnp.where(left, turned[1], b)])
            for k, slab in enumerate((slab_a, slab_b)):
                v = 4 * q + 2 * i + k
                packed[v] = slab.astype(jnp.bfloat16).reshape(6, 2, 4, LANES)
                owner = worker_of(v, parity)

                @pl.when(owner != me)
                def _():
                    pltpu.make_async_remote_copy(
                        src_ref=packed.at[v], dst_ref=held.at[me],
                        send_sem=out_sem, recv_sem=held_sem.at[me // half],
                        device_id=(block, owner), device_id_type=MESH,
                    ).start()

                @pl.when(owner == me)
                def _():
                    pltpu.make_async_copy(packed.at[v], held.at[me], held_sem.at[me // half]).start()

    for copy in smalls[1:]:
        copy.wait()
    inside = jnp.dot(marks, (first <= last).astype(f32).astype(jnp.bfloat16), preferred_element_type=f32)
    ahead = jnp.dot(ahead, one16, preferred_element_type=f32)
    slots = jnp.where(fluid > 0, (inside + ahead).astype(jnp.int32) - 1, -1)
    for t in range(tiles):
        here = jnp.broadcast_to(slots[t : t + 1, :], (LANES, LANES)).astype(i16)
        for i in range(spread.shape[0] // LANES):
            spread[i * LANES : (i + 1) * LANES, t * LANES : (t + 1) * LANES] = jnp.where(
                here == (first + i * LANES).astype(i16), one16, zero16
            )
    for r in range(shared // LANES):
        wanted = jnp.broadcast_to(send_v[r : r + 1, :], (LANES, LANES)).astype(i16)
        here = jnp.transpose(jnp.broadcast_to(recv_v[r : r + 1, :], (LANES, LANES))).astype(i16)
        for v in range(tiles):
            pick[v * LANES : (v + 1) * LANES, r * LANES : (r + 1) * LANES] = jnp.where(
                wanted == (first + v * LANES).astype(i16), one16, zero16
            )
            place[r * LANES : (r + 1) * LANES, v * LANES : (v + 1) * LANES] = jnp.where(
                here == (last + v * LANES).astype(i16), one16, zero16
            )
    digits = jnp.zeros((8, shared), f32)
    for v in range(tiles):
        number = jnp.broadcast_to(slots[v : v + 1, :], (8, LANES)) + 32
        digit = jnp.where(lax.broadcasted_iota(jnp.int32, (8, LANES), 0) == 0, number >> 5, number & 31)
        digits = digits + jnp.dot(
            digit.astype(f32).astype(jnp.bfloat16), pick[v * LANES : (v + 1) * LANES, :], preferred_element_type=f32
        )
    number = digits.astype(jnp.int32)
    number = number[0:1] * 32 + number[1:2] - 32
    for i in range(spread.shape[0] // LANES):
        row = lax.broadcasted_iota(jnp.int32, (LANES, shared), 0) + i * LANES
        chosen[i * LANES : (i + 1) * LANES, :] = jnp.where(number == row, 1.0, 0.0).astype(jnp.bfloat16)

    @pl.when(is_worker)
    def _():
        for copy in tables:
            copy.wait()
        turn_x, turn_y, turn_z = rot_s[0] * 2.0, rot_s[1] * 2.0, rot_s[2] * 2.0
        depth = half * 8
        rows = 16
        near = lax.broadcasted_iota(jnp.int32, (rows, LANES), 1) < LANES // 2
        turn_z = jnp.where(near, turn_z, 0.0)

        def arrived_modes(h):
            arrived = held.at[pl.ds(0, half)]
            pltpu.make_async_copy(arrived, arrived, held_sem.at[h]).wait()
            both = [held[h * half : (h + 1) * half, c].reshape(depth, LANES) for c in range(6)]
            return [jnp.concatenate(both[2 * q : 2 * q + 2], axis=1) for q in range(3)]

        for q, part in enumerate(arrived_modes(0)):
            phys[q] = jnp.dot(fwd_v[:, :depth], part, preferred_element_type=f32)

        late = arrived_modes(1)
        for k in range(3):
            third = slice(k * (angles // 3), (k + 1) * (angles // 3))
            for q in range(3):
                phys[q, third] = phys[q, third] + jnp.dot(
                    fwd_v[third, depth:], late[q], preferred_element_type=f32
                )
            for i in range(angles // 3 // rows):
                at = slice(third.start + i * rows, third.start + (i + 1) * rows)
                x = [phys[c // 2, at, (c % 2) * LANES : (c % 2 + 1) * LANES] for c in range(6)]
                cosine, sine = trig_v[0, at, :], trig_v[1, at, :]
                a, d = x[0:3], x[3:6]
                d = [d[0] + (turn_x * cosine + turn_y * sine), d[1] + (turn_y * cosine - turn_x * sine), d[2] + turn_z]
                e = [pltpu.roll(y, LANES // 2, 1) for y in a]
                for c in range(3):
                    m, n = (c + 1) % 3, (c + 2) % 3
                    force = a[m] * d[n] - a[n] * d[m]
                    force = force + pltpu.roll(force, LANES // 2, 1)
                    emf = e[m] * d[n] - e[n] * d[m]
                    prod[at, c * LANES : (c + 1) * LANES] = jnp.where(near, force, emf).astype(jnp.bfloat16)

        for h in range(2):
            back = jnp.dot(
                inv_v[h * depth : (h + 1) * depth, :], prod[...], preferred_element_type=f32
            ).astype(jnp.bfloat16)
            for c in range(3):
                spec[h * half : (h + 1) * half, c] = back[:, c * LANES : (c + 1) * LANES].reshape(half, 2, 4, LANES)

            def give(k, _):
                @pl.when(k != me)
                def _():
                    pltpu.make_async_remote_copy(
                        src_ref=spec.at[k], dst_ref=own.at[tile],
                        send_sem=back_out_sem, recv_sem=own_sem,
                        device_id=(block, k), device_id_type=MESH,
                    ).start()

                @pl.when(k == me)
                def _():
                    pltpu.make_async_copy(spec.at[k], own.at[tile], own_sem).start()

                return 0

            lax.fori_loop(h * half, (h + 1) * half, give, 0)

    pltpu.make_async_copy(own, own, own_sem).wait()
    for i in range(workers // 2):
        one, two = (own[2 * i + k].reshape(24, LANES).astype(f32) for k in range(2))
        force = jnp.where(left, one, pltpu.roll(two, LANES // 2, 1))
        emf = jnp.where(left, pltpu.roll(one, LANES // 2, 1), two)
        mine[:, i * LANES : (i + 1) * LANES] = jnp.concatenate([force, emf]).astype(jnp.bfloat16)
    picked[...] = jnp.dot(mine[...], chosen[...], preferred_element_type=f32).astype(jnp.bfloat16)
    swap = pltpu.make_async_remote_copy(
        src_ref=picked, dst_ref=given, send_sem=pair_out_sem, recv_sem=pair_in_sem,
        device_id=(partner, me), device_id_type=MESH,
    )
    swap.start()
    back = jnp.dot(mine[...], spread[...], preferred_element_type=f32)
    swap.wait_recv()
    step = nodes // 4
    writes = []
    for i in range(4):
        at = slice(i * step, (i + 1) * step)
        total = back[:, at] + jnp.dot(given[...], place[:, at], preferred_element_type=f32)
        result[i] = total.astype(jnp.bfloat16).reshape(6, 2, 4, step)
        writes.append(pltpu.make_async_copy(result.at[i], out.at[:, :, :, pl.ds(i * step, step)], done_sem.at[i]))
        writes[-1].start()
    for write in writes:
        write.wait()

    swap.wait_send()

    @pl.when(is_worker)
    def _():
        sent = packed.at[pl.ds(0, workers - 1)]
        pltpu.make_async_copy(sent, sent, out_sem).wait()
        gone = spec.at[pl.ds(0, groups - 1)]
        pltpu.make_async_copy(gone, gone, back_out_sem).wait()

    @pl.when(jnp.logical_not(is_worker))
    def _():
        pltpu.make_async_copy(packed, packed, out_sem).wait()


def body(velocity, vorticity, magnetic, current, rotation, fluid_label, send_rows, recv_rows):
    groups = lax.axis_size("fourier")
    comps, parts, local, nodes = velocity.shape
    modes = groups * local
    angles = 3 * modes
    tiles = nodes // LANES
    shared = send_rows.shape[1]
    forward, inverse = spectral_tables(modes, angles, groups)
    trig = angle_tables(angles)
    half16 = jnp.bfloat16
    any_ = pl.BlockSpec(memory_space=pltpu.HBM)
    workers = 16
    fluid_most = nodes // 2
    return pl.pallas_call(
        kernel,
        out_shape=jax.ShapeDtypeStruct((2 * comps, parts, local, nodes), half16),
        in_specs=[any_] * 11,
        out_specs=pl.BlockSpec(memory_space=pltpu.HBM),
        scratch_shapes=[
            pltpu.VMEM((4, comps, parts, local, nodes), half16),
            pltpu.VMEM((workers, 6, parts, local, LANES), half16),
            pltpu.VMEM((groups, 6, parts, local, LANES), half16),
            pltpu.VMEM((3, angles, 2 * LANES), jnp.float32),
            pltpu.VMEM((angles, 3 * LANES), half16),
            pltpu.VMEM((groups, 3, parts, local, LANES), half16),
            pltpu.VMEM((workers, 3, parts, local, LANES), half16),
            pltpu.VMEM((48, fluid_most), half16),
            pltpu.VMEM((48, shared), half16),
            pltpu.VMEM((48, shared), half16),
            pltpu.VMEM(forward.shape, half16),
            pltpu.VMEM(inverse.shape, half16),
            pltpu.VMEM(trig.shape, jnp.float32),
            pltpu.SMEM((3,), jnp.float32),
            pltpu.VMEM((tiles, LANES), jnp.int32),
            pltpu.VMEM((shared // LANES, LANES), jnp.int32),
            pltpu.VMEM((shared // LANES, LANES), jnp.int32),
            pltpu.VMEM((nodes, fluid_most), half16),
            pltpu.VMEM((nodes, shared), half16),
            pltpu.VMEM((fluid_most, shared), half16),
            pltpu.VMEM((shared, nodes), half16),
            pltpu.VMEM((fluid_most, nodes), half16),
            pltpu.SemaphoreType.DMA((7,)),
            pltpu.SemaphoreType.DMA((4,)),
            pltpu.SemaphoreType.DMA,
            pltpu.SemaphoreType.DMA((2,)),
            pltpu.SemaphoreType.DMA,
            pltpu.SemaphoreType.DMA,
            pltpu.SemaphoreType.DMA,
            pltpu.SemaphoreType.DMA,
            pltpu.VMEM((4, 2 * comps, parts, local, nodes // 4), half16),
            pltpu.SemaphoreType.DMA((4,)),
        ],
        compiler_params=pltpu.CompilerParams(
            collective_id=0, has_side_effects=True, vmem_limit_bytes=VMEM_BYTES
        ),
    )(
        velocity, vorticity, magnetic, current, rotation,
        fluid_label.reshape(tiles, LANES),
        send_rows.reshape(shared // LANES, LANES),
        recv_rows.reshape(shared // LANES, LANES),
        forward, inverse, trig,
    )


def solution(mesh):
    return jax.shard_map(
        body,
        mesh=mesh,
        in_specs=(
            P(None, None, "fourier", "mesh"),
            P(None, None, "fourier", "mesh"),
            P(None, None, "fourier", "mesh"),
            P(None, None, "fourier", "mesh"),
            P(),
            P("mesh"),
            P("mesh", None),
            P("mesh", None),
        ),
        out_specs=P(None, None, "fourier", "mesh"),
        check_vma=False,
    )
```

```python
import functools
import math

import jax
import jax.numpy as jnp
import ml_dtypes
import numpy as np
from jax import lax
from jax.experimental import pallas as pl
from jax.experimental.pallas import tpu as pltpu
from jax.sharding import PartitionSpec as P

MESH = pl.DeviceIdType.MESH
LANES = 128
VMEM_BYTES = 60 * 1024 * 1024
WORKERS = (
    (0, 2, 4, 6, 9, 11, 13, 15, 16, 18, 22, 25, 31, 32, 48, 56),
    (1, 3, 5, 7, 8, 10, 12, 14, 17, 19, 21, 23, 24, 30, 33, 40),
)
def spectral_tables(modes, angles, groups):
    index = np.arange(modes, dtype=np.int64)
    phase = (index[:, None] * np.arange(angles)[None, :] % angles).astype(np.float32)
    grid = phase * np.float32(2.0 * math.pi / angles)
    scaling = np.float32(1.0 / math.sqrt(angles))
    weight = np.where(index == 0, 1.0, 2.0).astype(np.float32)[:, None]
    forward = np.stack([weight * np.cos(grid), -weight * np.sin(grid)]) * scaling
    inverse = np.stack([np.cos(grid), -np.sin(grid)]) * scaling

    def by_owner(table):
        table = table.astype(ml_dtypes.bfloat16).reshape(2, groups, modes // groups, angles)
        return table.transpose(1, 0, 2, 3).reshape(2 * modes, angles)

    return np.ascontiguousarray(by_owner(forward).T), by_owner(inverse)


def angle_tables(angles):
    grid = np.arange(angles, dtype=np.float32) * np.float32(2.0 * math.pi / angles)
    wide = lambda a: np.ascontiguousarray(np.broadcast_to(a.astype(np.float32)[:, None], (angles, LANES)))
    both = np.stack([wide(np.cos(grid)), wide(np.sin(grid)), np.ones((angles, LANES), np.float32)])
    both[:, :, LANES // 2 :] = 0.0
    return both


def worker_of(v, parity):
    return jnp.where(parity == 0, WORKERS[0][v], WORKERS[1][v])


def kernel(
    vel, vor, mag, cur, rot, label, send, recv, fwd, inv, trig, out,
    fields, packed, held, phys, prod, spec, own, mine, picked, given,
    fwd_v, inv_v, trig_v, rot_s, label_v, send_v, recv_v, gather, pick, chosen, place, spread,
    load_sem, small_sem, out_sem, held_sem, back_out_sem, own_sem, pair_out_sem, pair_in_sem,
):
    block = lax.axis_index("mesh")
    me = lax.axis_index("fourier")
    groups = lax.axis_size("fourier")
    half = groups // 2
    parity = lax.rem(block, 2)
    partner = block + 1 - 2 * parity
    workers = own.shape[0]
    angles = fwd_v.shape[0]
    nodes = fields.shape[4]
    tiles = nodes // LANES
    shared = send_v.shape[0] * LANES

    tile = jnp.int32(0)
    works = jnp.int32(0)
    for v in range(workers):
        found = worker_of(v, parity) == me
        tile = tile + jnp.where(found, v, 0)
        works = works + jnp.where(found, 1, 0)
    is_worker = works > 0
    barrier = pltpu.get_barrier_semaphore()

    smalls = [
        pltpu.make_async_copy(label, label_v, small_sem.at[0]),
        pltpu.make_async_copy(send, send_v, small_sem.at[1]),
        pltpu.make_async_copy(recv, recv_v, small_sem.at[2]),
        pltpu.make_async_copy(rot, rot_s, small_sem.at[3]),
    ]
    loads = [
        pltpu.make_async_copy(field, fields.at[f], load_sem.at[3 + f]) for f, field in enumerate((vel, vor, mag, cur))
    ]
    tables = [
        pltpu.make_async_copy(fwd, fwd_v, load_sem.at[0]),
        pltpu.make_async_copy(inv, inv_v, load_sem.at[1]),
        pltpu.make_async_copy(trig, trig_v, load_sem.at[2]),
    ]
    for copy in smalls + loads:
        copy.start()

    @pl.when(is_worker)
    def _():
        def greet(i, _):
            pl.semaphore_signal(
                barrier, inc=1, device_id=(block, lax.rem(me + i, groups)), device_id_type=MESH
            )
            return 0

        lax.fori_loop(1, groups, greet, 0)
        for copy in tables:
            copy.start()

    pl.semaphore_signal(barrier, inc=1, device_id=(partner, me), device_id_type=MESH)

    f32 = jnp.float32
    i16 = jnp.int16
    smalls[0].wait()
    fluid = label_v[...]
    marks = fluid.astype(jnp.bfloat16)
    first = lax.broadcasted_iota(jnp.int32, (LANES, LANES), 0)
    last = lax.broadcasted_iota(jnp.int32, (LANES, LANES), 1)
    below = jnp.where(last < first, 2.0, jnp.where(last == first, 1.0, 0.0)).astype(jnp.bfloat16)
    before = lax.broadcasted_iota(jnp.int32, (tiles, tiles), 1) < lax.broadcasted_iota(jnp.int32, (tiles, tiles), 0)
    ahead = jnp.dot(before.astype(f32).astype(jnp.bfloat16), marks, preferred_element_type=f32).astype(jnp.bfloat16)
    across = (((1,), (1,)), ((), ()))
    code = lax.dot_general(below, marks, across, preferred_element_type=f32)
    code = code + lax.dot_general(
        jnp.full((LANES, LANES), 2.0, jnp.bfloat16), ahead, across, preferred_element_type=f32
    )
    code = code.astype(jnp.int32).astype(i16)

    for copy in loads:
        copy.wait()

    lines = fields.reshape(96, nodes)
    left = lax.broadcasted_iota(jnp.int32, (24, LANES), 1) < LANES // 2
    wide = 2 * LANES
    one16, zero16 = jnp.ones((LANES, LANES), jnp.bfloat16), jnp.zeros((LANES, LANES), jnp.bfloat16)
    for q in range(spread.shape[0] // wide):
        total = jnp.zeros((96, wide), f32)
        for t in range(q, tiles // 2):
            at = slice(t * wide, (t + 1) * wide)
            for n in (2 * t, 2 * t + 1):
                here = jnp.broadcast_to(code[:, n : n + 1], (LANES, LANES))
                for i in (2 * q, 2 * q + 1):
                    wanted = (last * 2 + (2 * i * LANES + 1)).astype(i16)
                    gather[n * LANES : (n + 1) * LANES, i * LANES : (i + 1) * LANES] = jnp.where(
                        here == wanted, one16, zero16
                    )
            total = total + jnp.dot(
                lines[:, at], gather[at, q * wide : (q + 1) * wide], preferred_element_type=f32
            )
        for i in range(2):
            part = total[:, i * LANES : (i + 1) * LANES]
            u, w, b, j = (part[24 * f : 24 * f + 24] for f in range(4))
            turned = [pltpu.roll(x, LANES // 2, 1) for x in (u, w, b, j)]
            slab_a = jnp.concatenate([jnp.where(left, u, turned[3]), jnp.where(left, w, turned[2])])
            slab_b = jnp.concatenate([jnp.where(left, turned[0], j), jnp.where(left, turned[1], b)])
            for k, slab in enumerate((slab_a, slab_b)):
                v = 4 * q + 2 * i + k
                packed[v] = slab.astype(jnp.bfloat16).reshape(6, 2, 4, LANES)

    def leave(v):
        return pltpu.make_async_remote_copy(
            src_ref=packed.at[v], dst_ref=held.at[me],
            send_sem=out_sem, recv_sem=held_sem.at[me // half],
            device_id=(block, worker_of(v, parity)), device_id_type=MESH,
        )

    @pl.when(jnp.logical_not(is_worker))
    def _():
        pl.semaphore_wait(barrier, workers + 1)
        for v in range(workers):
            leave(v).start()

    @pl.when(is_worker)
    def _():
        pl.semaphore_wait(barrier, workers)
        for v in range(workers):
            @pl.when(worker_of(v, parity) != me)
            def _():
                leave(v).start()

            @pl.when(worker_of(v, parity) == me)
            def _():
                pltpu.make_async_copy(packed.at[v], held.at[me], held_sem.at[me // half]).start()

    for copy in smalls[1:]:
        copy.wait()
    inside = jnp.dot(marks, (first <= last).astype(f32).astype(jnp.bfloat16), preferred_element_type=f32)
    ahead = jnp.dot(ahead, one16, preferred_element_type=f32)
    slots = jnp.where(fluid > 0, (inside + ahead).astype(jnp.int32) - 1, -1)
    for t in range(tiles):
        here = jnp.broadcast_to(slots[t : t + 1, :], (LANES, LANES)).astype(i16)
        for i in range(spread.shape[0] // LANES):
            spread[i * LANES : (i + 1) * LANES, t * LANES : (t + 1) * LANES] = jnp.where(
                here == (first + i * LANES).astype(i16), one16, zero16
            )
    for r in range(shared // LANES):
        wanted = jnp.broadcast_to(send_v[r : r + 1, :], (LANES, LANES)).astype(i16)
        here = jnp.transpose(jnp.broadcast_to(recv_v[r : r + 1, :], (LANES, LANES))).astype(i16)
        for v in range(tiles):
            pick[v * LANES : (v + 1) * LANES, r * LANES : (r + 1) * LANES] = jnp.where(
                wanted == (first + v * LANES).astype(i16), one16, zero16
            )
            place[r * LANES : (r + 1) * LANES, v * LANES : (v + 1) * LANES] = jnp.where(
                here == (last + v * LANES).astype(i16), one16, zero16
            )
    digits = jnp.zeros((8, shared), f32)
    for v in range(tiles):
        number = jnp.broadcast_to(slots[v : v + 1, :], (8, LANES)) + 32
        digit = jnp.where(lax.broadcasted_iota(jnp.int32, (8, LANES), 0) == 0, number >> 5, number & 31)
        digits = digits + jnp.dot(
            digit.astype(f32).astype(jnp.bfloat16), pick[v * LANES : (v + 1) * LANES, :], preferred_element_type=f32
        )
    number = digits.astype(jnp.int32)
    number = number[0:1] * 32 + number[1:2] - 32
    for i in range(spread.shape[0] // LANES):
        row = lax.broadcasted_iota(jnp.int32, (LANES, shared), 0) + i * LANES
        chosen[i * LANES : (i + 1) * LANES, :] = jnp.where(number == row, 1.0, 0.0).astype(jnp.bfloat16)

    @pl.when(is_worker)
    def _():
        for copy in tables:
            copy.wait()
        turn_x, turn_y, turn_z = rot_s[0] * 2.0, rot_s[1] * 2.0, rot_s[2] * 2.0
        depth = half * 8
        rows = 16
        near = lax.broadcasted_iota(jnp.int32, (rows, LANES), 1) < LANES // 2

        def arrived_modes(h):
            arrived = held.at[pl.ds(0, half)]
            pltpu.make_async_copy(arrived, arrived, held_sem.at[h]).wait()
            both = [held[h * half : (h + 1) * half, c].reshape(depth, LANES) for c in range(6)]
            return [jnp.concatenate(both[2 * q : 2 * q + 2], axis=1) for q in range(3)]

        cosine, sine = trig_v[0], trig_v[1]
        spin = [
            None, None, None,
            turn_x * cosine + turn_y * sine,
            turn_y * cosine - turn_x * sine,
            turn_z * trig_v[2],
        ]
        for q, part in enumerate(arrived_modes(0)):
            both = jnp.dot(fwd_v[:, :depth], part, preferred_element_type=f32)
            for i in range(2):
                lanes = slice(i * LANES, (i + 1) * LANES)
                turn = spin[2 * q + i]
                phys[q, :, lanes] = both[:, lanes] if turn is None else both[:, lanes] + turn

        late = arrived_modes(1)
        for k in range(3):
            third = slice(k * (angles // 3), (k + 1) * (angles // 3))
            for q in range(3):
                phys[q, third] = phys[q, third] + jnp.dot(
                    fwd_v[third, depth:], late[q], preferred_element_type=f32
                )
            for i in range(angles // 3 // rows):
                at = slice(third.start + i * rows, third.start + (i + 1) * rows)
                x = [phys[c // 2, at, (c % 2) * LANES : (c % 2 + 1) * LANES] for c in range(6)]
                a, d = x[0:3], x[3:6]
                e = [pltpu.roll(y, LANES // 2, 1) for y in a]
                for c in range(3):
                    m, n = (c + 1) % 3, (c + 2) % 3
                    force = a[m] * d[n] - a[n] * d[m]
                    force = force + pltpu.roll(force, LANES // 2, 1)
                    emf = e[m] * d[n] - e[n] * d[m]
                    prod[at, c * LANES : (c + 1) * LANES] = jnp.where(near, force, emf).astype(jnp.bfloat16)

        for begin, end in ((0, groups // 8), (groups // 8, half), (half, groups)):
            back = jnp.dot(
                inv_v[begin * 8 : end * 8, :], prod[...], preferred_element_type=f32
            ).astype(jnp.bfloat16)
            for c in range(3):
                spec[begin:end, c] = back[:, c * LANES : (c + 1) * LANES].reshape(end - begin, 2, 4, LANES)

            def give(k, _):
                @pl.when(k != me)
                def _():
                    pltpu.make_async_remote_copy(
                        src_ref=spec.at[k], dst_ref=own.at[tile],
                        send_sem=back_out_sem, recv_sem=own_sem,
                        device_id=(block, k), device_id_type=MESH,
                    ).start()

                @pl.when(k == me)
                def _():
                    pltpu.make_async_copy(spec.at[k], own.at[tile], own_sem).start()

                return 0

            lax.fori_loop(begin, end, give, 0)

    pltpu.make_async_copy(own, own, own_sem).wait()
    for i in range(workers // 2):
        one, two = (own[2 * i + k].reshape(24, LANES).astype(f32) for k in range(2))
        force = jnp.where(left, one, pltpu.roll(two, LANES // 2, 1))
        emf = jnp.where(left, pltpu.roll(one, LANES // 2, 1), two)
        mine[:, i * LANES : (i + 1) * LANES] = jnp.concatenate([force, emf]).astype(jnp.bfloat16)
    picked[...] = jnp.dot(mine[...], chosen[...], preferred_element_type=f32).astype(jnp.bfloat16)
    swap = pltpu.make_async_remote_copy(
        src_ref=picked, dst_ref=given, send_sem=pair_out_sem, recv_sem=pair_in_sem,
        device_id=(partner, me), device_id_type=MESH,
    )
    swap.start()
    back = jnp.dot(mine[...], spread[...], preferred_element_type=f32)
    swap.wait_recv()
    total = back + jnp.dot(given[...], place[...], preferred_element_type=f32)
    out[...] = total.astype(jnp.bfloat16).reshape(6, 2, 4, nodes)

    swap.wait_send()

    @pl.when(is_worker)
    def _():
        sent = packed.at[pl.ds(0, workers - 1)]
        pltpu.make_async_copy(sent, sent, out_sem).wait()
        gone = spec.at[pl.ds(0, groups - 1)]
        pltpu.make_async_copy(gone, gone, back_out_sem).wait()

    @pl.when(jnp.logical_not(is_worker))
    def _():
        pltpu.make_async_copy(packed, packed, out_sem).wait()


def body(velocity, vorticity, magnetic, current, rotation, fluid_label, send_rows, recv_rows):
    groups = lax.axis_size("fourier")
    comps, parts, local, nodes = velocity.shape
    modes = groups * local
    angles = 3 * modes
    tiles = nodes // LANES
    shared = send_rows.shape[1]
    forward, inverse = spectral_tables(modes, angles, groups)
    trig = angle_tables(angles)
    half16 = jnp.bfloat16
    any_ = pl.BlockSpec(memory_space=pltpu.HBM)
    workers = 16
    fluid_most = nodes // 2
    return pl.pallas_call(
        kernel,
        out_shape=pltpu.VMEM((2 * comps, parts, local, nodes), half16),
        in_specs=[any_] * 11,
        out_specs=pl.BlockSpec(memory_space=pltpu.VMEM),
        scratch_shapes=[
            pltpu.VMEM((4, comps, parts, local, nodes), half16),
            pltpu.VMEM((workers, 6, parts, local, LANES), half16),
            pltpu.VMEM((groups, 6, parts, local, LANES), half16),
            pltpu.VMEM((3, angles, 2 * LANES), jnp.float32),
            pltpu.VMEM((angles, 3 * LANES), half16),
            pltpu.VMEM((groups, 3, parts, local, LANES), half16),
            pltpu.VMEM((workers, 3, parts, local, LANES), half16),
            pltpu.VMEM((48, fluid_most), half16),
            pltpu.VMEM((48, shared), half16),
            pltpu.VMEM((48, shared), half16),
            pltpu.VMEM(forward.shape, half16),
            pltpu.VMEM(inverse.shape, half16),
            pltpu.VMEM(trig.shape, jnp.float32),
            pltpu.SMEM((3,), jnp.float32),
            pltpu.VMEM((tiles, LANES), jnp.int32),
            pltpu.VMEM((shared // LANES, LANES), jnp.int32),
            pltpu.VMEM((shared // LANES, LANES), jnp.int32),
            pltpu.VMEM((nodes, fluid_most), half16),
            pltpu.VMEM((nodes, shared), half16),
            pltpu.VMEM((fluid_most, shared), half16),
            pltpu.VMEM((shared, nodes), half16),
            pltpu.VMEM((fluid_most, nodes), half16),
            pltpu.SemaphoreType.DMA((7,)),
            pltpu.SemaphoreType.DMA((4,)),
            pltpu.SemaphoreType.DMA,
            pltpu.SemaphoreType.DMA((2,)),
            pltpu.SemaphoreType.DMA,
            pltpu.SemaphoreType.DMA,
            pltpu.SemaphoreType.DMA,
            pltpu.SemaphoreType.DMA,
        ],
        compiler_params=pltpu.CompilerParams(
            collective_id=0, has_side_effects=True, vmem_limit_bytes=VMEM_BYTES
        ),
    )(
        velocity, vorticity, magnetic, current, rotation,
        fluid_label.reshape(tiles, LANES),
        send_rows.reshape(shared // LANES, LANES),
        recv_rows.reshape(shared // LANES, LANES),
        forward, inverse, trig,
    )


def solution(mesh):
    return jax.shard_map(
        body,
        mesh=mesh,
        in_specs=(
            P(None, None, "fourier", "mesh"),
            P(None, None, "fourier", "mesh"),
            P(None, None, "fourier", "mesh"),
            P(None, None, "fourier", "mesh"),
            P(),
            P("mesh"),
            P("mesh", None),
            P("mesh", None),
        ),
        out_specs=P(None, None, "fourier", "mesh"),
        check_vma=False,
    )
```

```python
import functools
import math

import jax
import jax.numpy as jnp
import ml_dtypes
import numpy as np
from jax import lax
from jax.experimental import pallas as pl
from jax.experimental.pallas import tpu as pltpu
from jax.sharding import PartitionSpec as P

MESH = pl.DeviceIdType.MESH
LANES = 128
VMEM_BYTES = 60 * 1024 * 1024
WORKERS = (
    (0, 56, 2, 6, 9, 15, 16, 48, 4, 11, 13, 18, 22, 25, 31, 32),
    (1, 7, 8, 3, 5, 10, 14, 17, 23, 24, 40, 12, 19, 21, 26, 33),
)
NEAR = 12
def spectral_tables(modes, angles, groups):
    index = np.arange(modes, dtype=np.int64)
    phase = (index[:, None] * np.arange(angles)[None, :] % angles).astype(np.float32)
    grid = phase * np.float32(2.0 * math.pi / angles)
    scaling = np.float32(1.0 / math.sqrt(angles))
    weight = np.where(index == 0, 1.0, 2.0).astype(np.float32)[:, None]
    forward = np.stack([weight * np.cos(grid), -weight * np.sin(grid)]) * scaling
    inverse = np.stack([np.cos(grid), -np.sin(grid)]) * scaling

    def by_owner(table):
        table = table.astype(ml_dtypes.bfloat16).reshape(2, groups, modes // groups, angles)
        return table.transpose(1, 0, 2, 3).reshape(2 * modes, angles)

    return np.ascontiguousarray(by_owner(forward).T), by_owner(inverse)


def angle_tables(angles):
    grid = np.arange(angles, dtype=np.float32) * np.float32(2.0 * math.pi / angles)
    wide = lambda a: np.ascontiguousarray(np.broadcast_to(a.astype(np.float32)[:, None], (angles, LANES)))
    both = np.stack([wide(np.cos(grid)), wide(np.sin(grid)), np.ones((angles, LANES), np.float32)])
    both[:, :, LANES // 2 :] = 0.0
    return both


def worker_of(v, parity):
    return jnp.where(parity == 0, WORKERS[0][v], WORKERS[1][v])


def kernel(
    vel, vor, mag, cur, rot, label, send, recv, fwd, inv, trig, out,
    fields, packed, held, phys, prod, spec, own, mine, picked, given,
    fwd_v, inv_v, trig_v, rot_s, label_v, send_v, recv_v, gather, pick, chosen, place, spread,
    load_sem, small_sem, out_sem, held_sem, back_out_sem, own_sem, pair_out_sem, pair_in_sem,
):
    block = lax.axis_index("mesh")
    me = lax.axis_index("fourier")
    groups = lax.axis_size("fourier")
    half = groups // 2
    parity = lax.rem(block, 2)
    partner = block + 1 - 2 * parity
    workers = own.shape[0]
    angles = fwd_v.shape[0]
    nodes = fields.shape[4]
    tiles = nodes // LANES
    shared = send_v.shape[0] * LANES

    tile = jnp.int32(0)
    works = jnp.int32(0)
    for v in range(workers):
        found = worker_of(v, parity) == me
        tile = tile + jnp.where(found, v, 0)
        works = works + jnp.where(found, 1, 0)
    is_worker = works > 0
    side = jnp.where(tile < NEAR, 0, 1)
    barrier = pltpu.get_barrier_semaphore()

    smalls = [
        pltpu.make_async_copy(label, label_v, small_sem.at[0]),
        pltpu.make_async_copy(send, send_v, small_sem.at[1]),
        pltpu.make_async_copy(recv, recv_v, small_sem.at[2]),
        pltpu.make_async_copy(rot, rot_s, small_sem.at[3]),
    ]
    loads = [
        pltpu.make_async_copy(field, fields.at[f], load_sem.at[3 + f]) for f, field in enumerate((vel, vor, mag, cur))
    ]
    tables = [
        pltpu.make_async_copy(fwd, fwd_v, load_sem.at[0]),
        pltpu.make_async_copy(inv, inv_v, load_sem.at[1]),
        pltpu.make_async_copy(trig, trig_v, load_sem.at[2]),
    ]
    for copy in smalls + loads:
        copy.start()

    @pl.when(is_worker)
    def _():
        def greet(i, _):
            pl.semaphore_signal(
                barrier, inc=1, device_id=(block, lax.rem(me + i, groups)), device_id_type=MESH
            )
            return 0

        lax.fori_loop(1, groups, greet, 0)
        for copy in tables:
            copy.start()

    pl.semaphore_signal(barrier, inc=1, device_id=(partner, me), device_id_type=MESH)

    f32 = jnp.float32
    i16 = jnp.int16
    smalls[0].wait()
    fluid = label_v[...]
    marks = fluid.astype(jnp.bfloat16)
    first = lax.broadcasted_iota(jnp.int32, (LANES, LANES), 0)
    last = lax.broadcasted_iota(jnp.int32, (LANES, LANES), 1)
    below = jnp.where(last < first, 2.0, jnp.where(last == first, 1.0, 0.0)).astype(jnp.bfloat16)
    before = lax.broadcasted_iota(jnp.int32, (tiles, tiles), 1) < lax.broadcasted_iota(jnp.int32, (tiles, tiles), 0)
    ahead = jnp.dot(before.astype(f32).astype(jnp.bfloat16), marks, preferred_element_type=f32).astype(jnp.bfloat16)
    across = (((1,), (1,)), ((), ()))
    code = lax.dot_general(below, marks, across, preferred_element_type=f32)
    code = code + lax.dot_general(
        jnp.full((LANES, LANES), 2.0, jnp.bfloat16), ahead, across, preferred_element_type=f32
    )
    code = code.astype(jnp.int32).astype(i16)

    for copy in loads:
        copy.wait()

    lines = fields.reshape(96, nodes)
    left = lax.broadcasted_iota(jnp.int32, (24, LANES), 1) < LANES // 2
    wide = 2 * LANES
    one16, zero16 = jnp.ones((LANES, LANES), jnp.bfloat16), jnp.zeros((LANES, LANES), jnp.bfloat16)
    for q in range(spread.shape[0] // wide):
        total = jnp.zeros((96, wide), f32)
        for t in range(q, tiles // 2):
            at = slice(t * wide, (t + 1) * wide)
            for n in (2 * t, 2 * t + 1):
                here = jnp.broadcast_to(code[:, n : n + 1], (LANES, LANES))
                for i in (2 * q, 2 * q + 1):
                    wanted = (last * 2 + (2 * i * LANES + 1)).astype(i16)
                    gather[n * LANES : (n + 1) * LANES, i * LANES : (i + 1) * LANES] = jnp.where(
                        here == wanted, one16, zero16
                    )
            total = total + jnp.dot(
                lines[:, at], gather[at, q * wide : (q + 1) * wide], preferred_element_type=f32
            )
        for i in range(2):
            part = total[:, i * LANES : (i + 1) * LANES]
            u, w, b, j = (part[24 * f : 24 * f + 24] for f in range(4))
            turned = [pltpu.roll(x, LANES // 2, 1) for x in (u, w, b, j)]
            slab_a = jnp.concatenate([jnp.where(left, u, turned[3]), jnp.where(left, w, turned[2])])
            slab_b = jnp.concatenate([jnp.where(left, turned[0], j), jnp.where(left, turned[1], b)])
            for k, slab in enumerate((slab_a, slab_b)):
                v = 4 * q + 2 * i + k
                packed[v] = slab.astype(jnp.bfloat16).reshape(6, 2, 4, LANES)

    def leave(v):
        return pltpu.make_async_remote_copy(
            src_ref=packed.at[v], dst_ref=held.at[me],
            send_sem=out_sem, recv_sem=held_sem.at[me // half],
            device_id=(block, worker_of(v, parity)), device_id_type=MESH,
        )

    @pl.when(jnp.logical_not(is_worker))
    def _():
        pl.semaphore_wait(barrier, workers + 1)
        for v in range(workers):
            leave(v).start()

    @pl.when(is_worker)
    def _():
        pl.semaphore_wait(barrier, workers)
        for v in range(workers):
            @pl.when(worker_of(v, parity) != me)
            def _():
                leave(v).start()

            @pl.when(worker_of(v, parity) == me)
            def _():
                pltpu.make_async_copy(packed.at[v], held.at[me], held_sem.at[me // half]).start()

    for copy in smalls[1:]:
        copy.wait()
    inside = jnp.dot(marks, (first <= last).astype(f32).astype(jnp.bfloat16), preferred_element_type=f32)
    ahead = jnp.dot(ahead, one16, preferred_element_type=f32)
    slots = jnp.where(fluid > 0, (inside + ahead).astype(jnp.int32) - 1, -1)
    for t in range(tiles):
        here = jnp.broadcast_to(slots[t : t + 1, :], (LANES, LANES)).astype(i16)
        for i in range(spread.shape[0] // LANES):
            spread[i * LANES : (i + 1) * LANES, t * LANES : (t + 1) * LANES] = jnp.where(
                here == (first + i * LANES).astype(i16), one16, zero16
            )
    for r in range(shared // LANES):
        wanted = jnp.broadcast_to(send_v[r : r + 1, :], (LANES, LANES)).astype(i16)
        here = jnp.transpose(jnp.broadcast_to(recv_v[r : r + 1, :], (LANES, LANES))).astype(i16)
        for v in range(tiles):
            pick[v * LANES : (v + 1) * LANES, r * LANES : (r + 1) * LANES] = jnp.where(
                wanted == (first + v * LANES).astype(i16), one16, zero16
            )
            place[r * LANES : (r + 1) * LANES, v * LANES : (v + 1) * LANES] = jnp.where(
                here == (last + v * LANES).astype(i16), one16, zero16
            )
    digits = jnp.zeros((8, shared), f32)
    for v in range(tiles):
        number = jnp.broadcast_to(slots[v : v + 1, :], (8, LANES)) + 32
        digit = jnp.where(lax.broadcasted_iota(jnp.int32, (8, LANES), 0) == 0, number >> 5, number & 31)
        digits = digits + jnp.dot(
            digit.astype(f32).astype(jnp.bfloat16), pick[v * LANES : (v + 1) * LANES, :], preferred_element_type=f32
        )
    number = digits.astype(jnp.int32)
    number = number[0:1] * 32 + number[1:2] - 32
    for i in range(spread.shape[0] // LANES):
        row = lax.broadcasted_iota(jnp.int32, (LANES, shared), 0) + i * LANES
        chosen[i * LANES : (i + 1) * LANES, :] = jnp.where(number == row, 1.0, 0.0).astype(jnp.bfloat16)

    @pl.when(is_worker)
    def _():
        for copy in tables:
            copy.wait()
        turn_x, turn_y, turn_z = rot_s[0] * 2.0, rot_s[1] * 2.0, rot_s[2] * 2.0
        depth = half * 8
        rows = 16
        near = lax.broadcasted_iota(jnp.int32, (rows, LANES), 1) < LANES // 2

        def arrived_modes(h):
            arrived = held.at[pl.ds(0, half)]
            pltpu.make_async_copy(arrived, arrived, held_sem.at[h]).wait()
            both = [held[h * half : (h + 1) * half, c].reshape(depth, LANES) for c in range(6)]
            return [jnp.concatenate(both[2 * q : 2 * q + 2], axis=1) for q in range(3)]

        cosine, sine = trig_v[0], trig_v[1]
        spin = [
            None, None, None,
            turn_x * cosine + turn_y * sine,
            turn_y * cosine - turn_x * sine,
            turn_z * trig_v[2],
        ]
        for q, part in enumerate(arrived_modes(0)):
            both = jnp.dot(fwd_v[:, :depth], part, preferred_element_type=f32)
            for i in range(2):
                lanes = slice(i * LANES, (i + 1) * LANES)
                turn = spin[2 * q + i]
                phys[q, :, lanes] = both[:, lanes] if turn is None else both[:, lanes] + turn

        late = arrived_modes(1)
        for k in range(3):
            third = slice(k * (angles // 3), (k + 1) * (angles // 3))
            for q in range(3):
                phys[q, third] = phys[q, third] + jnp.dot(
                    fwd_v[third, depth:], late[q], preferred_element_type=f32
                )
            for i in range(angles // 3 // rows):
                at = slice(third.start + i * rows, third.start + (i + 1) * rows)
                x = [phys[c // 2, at, (c % 2) * LANES : (c % 2 + 1) * LANES] for c in range(6)]
                a, d = x[0:3], x[3:6]
                e = [pltpu.roll(y, LANES // 2, 1) for y in a]
                for c in range(3):
                    m, n = (c + 1) % 3, (c + 2) % 3
                    force = a[m] * d[n] - a[n] * d[m]
                    force = force + pltpu.roll(force, LANES // 2, 1)
                    emf = e[m] * d[n] - e[n] * d[m]
                    prod[at, c * LANES : (c + 1) * LANES] = jnp.where(near, force, emf).astype(jnp.bfloat16)

        for begin, end in ((0, groups // 8), (groups // 8, half), (half, groups)):
            back = jnp.dot(
                inv_v[begin * 8 : end * 8, :], prod[...], preferred_element_type=f32
            ).astype(jnp.bfloat16)
            for c in range(3):
                spec[begin:end, c] = back[:, c * LANES : (c + 1) * LANES].reshape(end - begin, 2, 4, LANES)

            def give(k, _):
                @pl.when(k != me)
                def _():
                    pltpu.make_async_remote_copy(
                        src_ref=spec.at[k], dst_ref=own.at[tile],
                        send_sem=back_out_sem, recv_sem=own_sem.at[side],
                        device_id=(block, k), device_id_type=MESH,
                    ).start()

                @pl.when(k == me)
                def _():
                    pltpu.make_async_copy(spec.at[k], own.at[tile], own_sem.at[side]).start()

                return 0

            lax.fori_loop(begin, end, give, 0)

    columns = shared // 2
    chosen_sum = back = None
    swaps = []
    for g, (begin, end) in enumerate(((0, NEAR), (NEAR, workers))):
        come = own.at[pl.ds(begin, end - begin)]
        pltpu.make_async_copy(come, come, own_sem.at[g]).wait()
        for i in range(begin // 2, end // 2):
            one, two = (own[2 * i + k].reshape(24, LANES).astype(f32) for k in range(2))
            force = jnp.where(left, one, pltpu.roll(two, LANES // 2, 1))
            emf = jnp.where(left, pltpu.roll(one, LANES // 2, 1), two)
            mine[:, i * LANES : (i + 1) * LANES] = jnp.concatenate([force, emf]).astype(jnp.bfloat16)
        at = slice(begin * LANES // 2, end * LANES // 2)
        if g == 0:
            chosen_sum = jnp.dot(mine[:, at], chosen[at, :], preferred_element_type=f32)
            back = jnp.dot(mine[:, at], spread[at, :], preferred_element_type=f32)
        else:
            for h in range(2):
                lanes = slice(h * columns, (h + 1) * columns)
                part = jnp.dot(mine[:, at], chosen[at, lanes], preferred_element_type=f32)
                picked[h] = (chosen_sum[:, lanes] + part).astype(jnp.bfloat16)
                swaps.append(
                    pltpu.make_async_remote_copy(
                        src_ref=picked.at[h], dst_ref=given.at[h],
                        send_sem=pair_out_sem.at[h], recv_sem=pair_in_sem.at[h],
                        device_id=(partner, me), device_id_type=MESH,
                    )
                )
                swaps[h].start()
            back = back + jnp.dot(mine[:, at], spread[at, :], preferred_element_type=f32)
    for h in range(2):
        swaps[h].wait_recv()
        back = back + jnp.dot(
            given[h], place[h * columns : (h + 1) * columns, :], preferred_element_type=f32
        )
    out[...] = back.astype(jnp.bfloat16).reshape(6, 2, 4, nodes)

    for swap in swaps:
        swap.wait_send()

    @pl.when(is_worker)
    def _():
        sent = packed.at[pl.ds(0, workers - 1)]
        pltpu.make_async_copy(sent, sent, out_sem).wait()
        gone = spec.at[pl.ds(0, groups - 1)]
        pltpu.make_async_copy(gone, gone, back_out_sem).wait()

    @pl.when(jnp.logical_not(is_worker))
    def _():
        pltpu.make_async_copy(packed, packed, out_sem).wait()


def body(velocity, vorticity, magnetic, current, rotation, fluid_label, send_rows, recv_rows):
    groups = lax.axis_size("fourier")
    comps, parts, local, nodes = velocity.shape
    modes = groups * local
    angles = 3 * modes
    tiles = nodes // LANES
    shared = send_rows.shape[1]
    forward, inverse = spectral_tables(modes, angles, groups)
    trig = angle_tables(angles)
    half16 = jnp.bfloat16
    any_ = pl.BlockSpec(memory_space=pltpu.HBM)
    workers = 16
    fluid_most = nodes // 2
    return pl.pallas_call(
        kernel,
        out_shape=pltpu.VMEM((2 * comps, parts, local, nodes), half16),
        in_specs=[any_] * 11,
        out_specs=pl.BlockSpec(memory_space=pltpu.VMEM),
        scratch_shapes=[
            pltpu.VMEM((4, comps, parts, local, nodes), half16),
            pltpu.VMEM((workers, 6, parts, local, LANES), half16),
            pltpu.VMEM((groups, 6, parts, local, LANES), half16),
            pltpu.VMEM((3, angles, 2 * LANES), jnp.float32),
            pltpu.VMEM((angles, 3 * LANES), half16),
            pltpu.VMEM((groups, 3, parts, local, LANES), half16),
            pltpu.VMEM((workers, 3, parts, local, LANES), half16),
            pltpu.VMEM((48, fluid_most), half16),
            pltpu.VMEM((2, 48, shared // 2), half16),
            pltpu.VMEM((2, 48, shared // 2), half16),
            pltpu.VMEM(forward.shape, half16),
            pltpu.VMEM(inverse.shape, half16),
            pltpu.VMEM(trig.shape, jnp.float32),
            pltpu.SMEM((3,), jnp.float32),
            pltpu.VMEM((tiles, LANES), jnp.int32),
            pltpu.VMEM((shared // LANES, LANES), jnp.int32),
            pltpu.VMEM((shared // LANES, LANES), jnp.int32),
            pltpu.VMEM((nodes, fluid_most), half16),
            pltpu.VMEM((nodes, shared), half16),
            pltpu.VMEM((fluid_most, shared), half16),
            pltpu.VMEM((shared, nodes), half16),
            pltpu.VMEM((fluid_most, nodes), half16),
            pltpu.SemaphoreType.DMA((7,)),
            pltpu.SemaphoreType.DMA((4,)),
            pltpu.SemaphoreType.DMA,
            pltpu.SemaphoreType.DMA((2,)),
            pltpu.SemaphoreType.DMA,
            pltpu.SemaphoreType.DMA((2,)),
            pltpu.SemaphoreType.DMA((2,)),
            pltpu.SemaphoreType.DMA((2,)),
        ],
        compiler_params=pltpu.CompilerParams(
            collective_id=0, has_side_effects=True, vmem_limit_bytes=VMEM_BYTES
        ),
    )(
        velocity, vorticity, magnetic, current, rotation,
        fluid_label.reshape(tiles, LANES),
        send_rows.reshape(shared // LANES, LANES),
        recv_rows.reshape(shared // LANES, LANES),
        forward, inverse, trig,
    )


def solution(mesh):
    return jax.shard_map(
        body,
        mesh=mesh,
        in_specs=(
            P(None, None, "fourier", "mesh"),
            P(None, None, "fourier", "mesh"),
            P(None, None, "fourier", "mesh"),
            P(None, None, "fourier", "mesh"),
            P(),
            P("mesh"),
            P("mesh", None),
            P("mesh", None),
        ),
        out_specs=P(None, None, "fourier", "mesh"),
        check_vma=False,
    )
```

```python
import functools
import math

import jax
import jax.numpy as jnp
import ml_dtypes
import numpy as np
from jax import lax
from jax.experimental import pallas as pl
from jax.experimental.pallas import tpu as pltpu
from jax.sharding import PartitionSpec as P

MESH = pl.DeviceIdType.MESH
LANES = 128
VMEM_BYTES = 60 * 1024 * 1024
WORKERS = (
    (0, 56, 2, 6, 9, 15, 16, 48, 4, 11, 13, 18, 22, 25, 31, 32),
    (1, 7, 8, 3, 5, 10, 14, 17, 23, 24, 40, 12, 19, 21, 26, 33),
)
NEAR = 12
def spectral_tables(modes, angles, groups):
    index = np.arange(modes, dtype=np.int64)
    phase = (index[:, None] * np.arange(angles)[None, :] % angles).astype(np.float32)
    grid = phase * np.float32(2.0 * math.pi / angles)
    scaling = np.float32(1.0 / math.sqrt(angles))
    weight = np.where(index == 0, 1.0, 2.0).astype(np.float32)[:, None]
    forward = np.stack([weight * np.cos(grid), -weight * np.sin(grid)]) * scaling
    inverse = np.stack([np.cos(grid), -np.sin(grid)]) * scaling

    def by_owner(table):
        table = table.astype(ml_dtypes.bfloat16).reshape(2, groups, modes // groups, angles)
        return table.transpose(1, 0, 2, 3).reshape(2 * modes, angles)

    return np.ascontiguousarray(by_owner(forward).T), by_owner(inverse)


def angle_tables(angles):
    grid = np.arange(angles, dtype=np.float32) * np.float32(2.0 * math.pi / angles)
    wide = lambda a: np.ascontiguousarray(np.broadcast_to(a.astype(np.float32)[:, None], (angles, LANES)))
    both = np.stack([wide(np.cos(grid)), wide(np.sin(grid)), np.ones((angles, LANES), np.float32)])
    both[:, :, LANES // 2 :] = 0.0
    return both


def worker_of(v, parity):
    return jnp.where(parity == 0, WORKERS[0][v], WORKERS[1][v])


def kernel(
    vel, vor, mag, cur, rot, label, send, recv, fwd, inv, trig, out,
    fields, packed, held, phys, prod, spec, own, mine, picked, given,
    fwd_v, inv_v, trig_v, rot_s, label_v, send_v, recv_v, gather, pick, chosen, place, spread,
    load_sem, small_sem, out_sem, held_sem, back_out_sem, own_sem, pair_out_sem, pair_in_sem,
):
    block = lax.axis_index("mesh")
    me = lax.axis_index("fourier")
    groups = lax.axis_size("fourier")
    half = groups // 2
    parity = lax.rem(block, 2)
    partner = block + 1 - 2 * parity
    workers = own.shape[0]
    angles = fwd_v.shape[0]
    nodes = fields.shape[4]
    tiles = nodes // LANES
    shared = send_v.shape[0] * LANES

    tile = jnp.int32(0)
    works = jnp.int32(0)
    for v in range(workers):
        found = worker_of(v, parity) == me
        tile = tile + jnp.where(found, v, 0)
        works = works + jnp.where(found, 1, 0)
    is_worker = works > 0
    side = jnp.where(tile < NEAR, 0, 1)
    barrier = pltpu.get_barrier_semaphore()

    smalls = [
        pltpu.make_async_copy(label, label_v, small_sem.at[0]),
        pltpu.make_async_copy(send, send_v, small_sem.at[1]),
        pltpu.make_async_copy(recv, recv_v, small_sem.at[2]),
        pltpu.make_async_copy(rot, rot_s, small_sem.at[3]),
    ]
    loads = [
        pltpu.make_async_copy(field, fields.at[f], load_sem.at[3 + f]) for f, field in enumerate((vel, vor, mag, cur))
    ]
    tables = [
        pltpu.make_async_copy(fwd, fwd_v, load_sem.at[0]),
        pltpu.make_async_copy(inv, inv_v, load_sem.at[1]),
        pltpu.make_async_copy(trig, trig_v, load_sem.at[2]),
    ]
    for copy in smalls + loads:
        copy.start()

    @pl.when(is_worker)
    def _():
        def greet(i, _):
            pl.semaphore_signal(
                barrier, inc=1, device_id=(block, lax.rem(me + i, groups)), device_id_type=MESH
            )
            return 0

        lax.fori_loop(1, groups, greet, 0, unroll=9)
        for copy in tables:
            copy.start()

    pl.semaphore_signal(barrier, inc=1, device_id=(partner, me), device_id_type=MESH)

    f32 = jnp.float32
    i16 = jnp.int16
    smalls[0].wait()
    fluid = label_v[...]
    marks = fluid.astype(jnp.bfloat16)
    first = lax.broadcasted_iota(jnp.int32, (LANES, LANES), 0)
    last = lax.broadcasted_iota(jnp.int32, (LANES, LANES), 1)
    below = jnp.where(last < first, 2.0, jnp.where(last == first, 1.0, 0.0)).astype(jnp.bfloat16)
    before = lax.broadcasted_iota(jnp.int32, (tiles, tiles), 1) < lax.broadcasted_iota(jnp.int32, (tiles, tiles), 0)
    ahead = jnp.dot(before.astype(f32).astype(jnp.bfloat16), marks, preferred_element_type=f32).astype(jnp.bfloat16)
    across = (((1,), (1,)), ((), ()))
    code = lax.dot_general(below, marks, across, preferred_element_type=f32)
    code = code + lax.dot_general(
        jnp.full((LANES, LANES), 2.0, jnp.bfloat16), ahead, across, preferred_element_type=f32
    )
    code = code.astype(jnp.int32).astype(i16)

    for copy in loads:
        copy.wait()

    lines = fields.reshape(96, nodes)
    left = lax.broadcasted_iota(jnp.int32, (24, LANES), 1) < LANES // 2
    wide = 2 * LANES
    one16, zero16 = jnp.ones((LANES, LANES), jnp.bfloat16), jnp.zeros((LANES, LANES), jnp.bfloat16)
    for q in range(spread.shape[0] // wide):
        total = jnp.zeros((96, wide), f32)
        for t in range(q, tiles // 2):
            at = slice(t * wide, (t + 1) * wide)
            for n in (2 * t, 2 * t + 1):
                here = jnp.broadcast_to(code[:, n : n + 1], (LANES, LANES))
                for i in (2 * q, 2 * q + 1):
                    wanted = (last * 2 + (2 * i * LANES + 1)).astype(i16)
                    gather[n * LANES : (n + 1) * LANES, i * LANES : (i + 1) * LANES] = jnp.where(
                        here == wanted, one16, zero16
                    )
            total = total + jnp.dot(
                lines[:, at], gather[at, q * wide : (q + 1) * wide], preferred_element_type=f32
            )
        for i in range(2):
            part = total[:, i * LANES : (i + 1) * LANES]
            u, w, b, j = (part[24 * f : 24 * f + 24] for f in range(4))
            turned = [pltpu.roll(x, LANES // 2, 1) for x in (u, w, b, j)]
            slab_a = jnp.concatenate([jnp.where(left, u, turned[3]), jnp.where(left, w, turned[2])])
            slab_b = jnp.concatenate([jnp.where(left, turned[0], j), jnp.where(left, turned[1], b)])
            for k, slab in enumerate((slab_a, slab_b)):
                v = 4 * q + 2 * i + k
                packed[v] = slab.astype(jnp.bfloat16).reshape(6, 2, 4, LANES)

    def leave(v):
        return pltpu.make_async_remote_copy(
            src_ref=packed.at[v], dst_ref=held.at[me],
            send_sem=out_sem, recv_sem=held_sem.at[me // half],
            device_id=(block, worker_of(v, parity)), device_id_type=MESH,
        )

    @pl.when(jnp.logical_not(is_worker))
    def _():
        pl.semaphore_wait(barrier, workers + 1)
        for v in range(workers):
            leave(v).start()

    @pl.when(is_worker)
    def _():
        pl.semaphore_wait(barrier, workers)
        for v in range(workers):
            @pl.when(worker_of(v, parity) != me)
            def _():
                leave(v).start()

            @pl.when(worker_of(v, parity) == me)
            def _():
                pltpu.make_async_copy(packed.at[v], held.at[me], held_sem.at[me // half]).start()

    for copy in smalls[1:]:
        copy.wait()
    inside = jnp.dot(marks, (first <= last).astype(f32).astype(jnp.bfloat16), preferred_element_type=f32)
    ahead = jnp.dot(ahead, one16, preferred_element_type=f32)
    slots = jnp.where(fluid > 0, (inside + ahead).astype(jnp.int32) - 1, -1)
    for t in range(tiles):
        here = jnp.broadcast_to(slots[t : t + 1, :], (LANES, LANES)).astype(i16)
        for i in range(spread.shape[0] // LANES):
            spread[i * LANES : (i + 1) * LANES, t * LANES : (t + 1) * LANES] = jnp.where(
                here == (first + i * LANES).astype(i16), one16, zero16
            )
    for r in range(shared // LANES):
        wanted = jnp.broadcast_to(send_v[r : r + 1, :], (LANES, LANES)).astype(i16)
        here = jnp.transpose(jnp.broadcast_to(recv_v[r : r + 1, :], (LANES, LANES))).astype(i16)
        for v in range(tiles):
            pick[v * LANES : (v + 1) * LANES, r * LANES : (r + 1) * LANES] = jnp.where(
                wanted == (first + v * LANES).astype(i16), one16, zero16
            )
            place[r * LANES : (r + 1) * LANES, v * LANES : (v + 1) * LANES] = jnp.where(
                here == (last + v * LANES).astype(i16), one16, zero16
            )
    digits = jnp.zeros((8, shared), f32)
    for v in range(tiles):
        number = jnp.broadcast_to(slots[v : v + 1, :], (8, LANES)) + 32
        digit = jnp.where(lax.broadcasted_iota(jnp.int32, (8, LANES), 0) == 0, number >> 5, number & 31)
        digits = digits + jnp.dot(
            digit.astype(f32).astype(jnp.bfloat16), pick[v * LANES : (v + 1) * LANES, :], preferred_element_type=f32
        )
    number = digits.astype(jnp.int32)
    number = number[0:1] * 32 + number[1:2] - 32
    for i in range(spread.shape[0] // LANES):
        row = lax.broadcasted_iota(jnp.int32, (LANES, shared), 0) + i * LANES
        chosen[i * LANES : (i + 1) * LANES, :] = jnp.where(number == row, 1.0, 0.0).astype(jnp.bfloat16)

    @pl.when(is_worker)
    def _():
        for copy in tables:
            copy.wait()
        turn_x, turn_y, turn_z = rot_s[0] * 2.0, rot_s[1] * 2.0, rot_s[2] * 2.0
        depth = half * 8
        rows = 16
        near = lax.broadcasted_iota(jnp.int32, (rows, LANES), 1) < LANES // 2

        def arrived_modes(h):
            arrived = held.at[pl.ds(0, half)]
            pltpu.make_async_copy(arrived, arrived, held_sem.at[h]).wait()
            both = [held[h * half : (h + 1) * half, c].reshape(depth, LANES) for c in range(6)]
            return [jnp.concatenate(both[2 * q : 2 * q + 2], axis=1) for q in range(3)]

        cosine, sine = trig_v[0], trig_v[1]
        spin = [
            None, None, None,
            turn_x * cosine + turn_y * sine,
            turn_y * cosine - turn_x * sine,
            turn_z * trig_v[2],
        ]
        for q, part in enumerate(arrived_modes(0)):
            both = jnp.dot(fwd_v[:, :depth], part, preferred_element_type=f32)
            for i in range(2):
                lanes = slice(i * LANES, (i + 1) * LANES)
                turn = spin[2 * q + i]
                phys[q, :, lanes] = both[:, lanes] if turn is None else both[:, lanes] + turn

        late = arrived_modes(1)
        for k in range(3):
            third = slice(k * (angles // 3), (k + 1) * (angles // 3))
            for q in range(3):
                phys[q, third] = phys[q, third] + jnp.dot(
                    fwd_v[third, depth:], late[q], preferred_element_type=f32
                )
            for i in range(angles // 3 // rows):
                at = slice(third.start + i * rows, third.start + (i + 1) * rows)
                x = [phys[c // 2, at, (c % 2) * LANES : (c % 2 + 1) * LANES] for c in range(6)]
                a, d = x[0:3], x[3:6]
                e = [pltpu.roll(y, LANES // 2, 1) for y in a]
                for c in range(3):
                    m, n = (c + 1) % 3, (c + 2) % 3
                    force = a[m] * d[n] - a[n] * d[m]
                    force = force + pltpu.roll(force, LANES // 2, 1)
                    emf = e[m] * d[n] - e[n] * d[m]
                    prod[at, c * LANES : (c + 1) * LANES] = jnp.where(near, force, emf).astype(jnp.bfloat16)

        for begin, end in ((0, groups // 8), (groups // 8, half), (half, groups)):
            back = jnp.dot(
                inv_v[begin * 8 : end * 8, :], prod[...], preferred_element_type=f32
            ).astype(jnp.bfloat16)
            for c in range(3):
                spec[begin:end, c] = back[:, c * LANES : (c + 1) * LANES].reshape(end - begin, 2, 4, LANES)

            def give(k, _):
                @pl.when(k != me)
                def _():
                    pltpu.make_async_remote_copy(
                        src_ref=spec.at[k], dst_ref=own.at[tile],
                        send_sem=back_out_sem, recv_sem=own_sem.at[side],
                        device_id=(block, k), device_id_type=MESH,
                    ).start()

                @pl.when(k == me)
                def _():
                    pltpu.make_async_copy(spec.at[k], own.at[tile], own_sem.at[side]).start()

                return 0

            lax.fori_loop(begin, end, give, 0, unroll=8)

    columns = shared // 2
    chosen_sum = back = None
    swaps = []
    for g, (begin, end) in enumerate(((0, NEAR), (NEAR, workers))):
        come = own.at[pl.ds(begin, end - begin)]
        pltpu.make_async_copy(come, come, own_sem.at[g]).wait()
        for i in range(begin // 2, end // 2):
            one, two = (own[2 * i + k].reshape(24, LANES).astype(f32) for k in range(2))
            force = jnp.where(left, one, pltpu.roll(two, LANES // 2, 1))
            emf = jnp.where(left, pltpu.roll(one, LANES // 2, 1), two)
            mine[:, i * LANES : (i + 1) * LANES] = jnp.concatenate([force, emf]).astype(jnp.bfloat16)
        at = slice(begin * LANES // 2, end * LANES // 2)
        if g == 0:
            chosen_sum = jnp.dot(mine[:, at], chosen[at, :], preferred_element_type=f32)
            back = jnp.dot(mine[:, at], spread[at, :], preferred_element_type=f32)
        else:
            for h in range(2):
                lanes = slice(h * columns, (h + 1) * columns)
                part = jnp.dot(mine[:, at], chosen[at, lanes], preferred_element_type=f32)
                picked[h] = (chosen_sum[:, lanes] + part).astype(jnp.bfloat16)
                swaps.append(
                    pltpu.make_async_remote_copy(
                        src_ref=picked.at[h], dst_ref=given.at[h],
                        send_sem=pair_out_sem.at[h], recv_sem=pair_in_sem.at[h],
                        device_id=(partner, me), device_id_type=MESH,
                    )
                )
                swaps[h].start()
            back = back + jnp.dot(mine[:, at], spread[at, :], preferred_element_type=f32)
    for h in range(2):
        swaps[h].wait_recv()
        back = back + jnp.dot(
            given[h], place[h * columns : (h + 1) * columns, :], preferred_element_type=f32
        )
    out[...] = back.astype(jnp.bfloat16).reshape(6, 2, 4, nodes)

    for swap in swaps:
        swap.wait_send()

    @pl.when(is_worker)
    def _():
        sent = packed.at[pl.ds(0, workers - 1)]
        pltpu.make_async_copy(sent, sent, out_sem).wait()
        gone = spec.at[pl.ds(0, groups - 1)]
        pltpu.make_async_copy(gone, gone, back_out_sem).wait()

    @pl.when(jnp.logical_not(is_worker))
    def _():
        pltpu.make_async_copy(packed, packed, out_sem).wait()


def body(velocity, vorticity, magnetic, current, rotation, fluid_label, send_rows, recv_rows):
    groups = lax.axis_size("fourier")
    comps, parts, local, nodes = velocity.shape
    modes = groups * local
    angles = 3 * modes
    tiles = nodes // LANES
    shared = send_rows.shape[1]
    forward, inverse = spectral_tables(modes, angles, groups)
    trig = angle_tables(angles)
    half16 = jnp.bfloat16
    any_ = pl.BlockSpec(memory_space=pltpu.HBM)
    workers = 16
    fluid_most = nodes // 2
    return pl.pallas_call(
        kernel,
        out_shape=pltpu.VMEM((2 * comps, parts, local, nodes), half16),
        in_specs=[any_] * 11,
        out_specs=pl.BlockSpec(memory_space=pltpu.VMEM),
        scratch_shapes=[
            pltpu.VMEM((4, comps, parts, local, nodes), half16),
            pltpu.VMEM((workers, 6, parts, local, LANES), half16),
            pltpu.VMEM((groups, 6, parts, local, LANES), half16),
            pltpu.VMEM((3, angles, 2 * LANES), jnp.float32),
            pltpu.VMEM((angles, 3 * LANES), half16),
            pltpu.VMEM((groups, 3, parts, local, LANES), half16),
            pltpu.VMEM((workers, 3, parts, local, LANES), half16),
            pltpu.VMEM((48, fluid_most), half16),
            pltpu.VMEM((2, 48, shared // 2), half16),
            pltpu.VMEM((2, 48, shared // 2), half16),
            pltpu.VMEM(forward.shape, half16),
            pltpu.VMEM(inverse.shape, half16),
            pltpu.VMEM(trig.shape, jnp.float32),
            pltpu.SMEM((3,), jnp.float32),
            pltpu.VMEM((tiles, LANES), jnp.int32),
            pltpu.VMEM((shared // LANES, LANES), jnp.int32),
            pltpu.VMEM((shared // LANES, LANES), jnp.int32),
            pltpu.VMEM((nodes, fluid_most), half16),
            pltpu.VMEM((nodes, shared), half16),
            pltpu.VMEM((fluid_most, shared), half16),
            pltpu.VMEM((shared, nodes), half16),
            pltpu.VMEM((fluid_most, nodes), half16),
            pltpu.SemaphoreType.DMA((7,)),
            pltpu.SemaphoreType.DMA((4,)),
            pltpu.SemaphoreType.DMA,
            pltpu.SemaphoreType.DMA((2,)),
            pltpu.SemaphoreType.DMA,
            pltpu.SemaphoreType.DMA((2,)),
            pltpu.SemaphoreType.DMA((2,)),
            pltpu.SemaphoreType.DMA((2,)),
        ],
        compiler_params=pltpu.CompilerParams(
            collective_id=0, has_side_effects=True, vmem_limit_bytes=VMEM_BYTES
        ),
    )(
        velocity, vorticity, magnetic, current, rotation,
        fluid_label.reshape(tiles, LANES),
        send_rows.reshape(shared // LANES, LANES),
        recv_rows.reshape(shared // LANES, LANES),
        forward, inverse, trig,
    )


def solution(mesh):
    return jax.shard_map(
        body,
        mesh=mesh,
        in_specs=(
            P(None, None, "fourier", "mesh"),
            P(None, None, "fourier", "mesh"),
            P(None, None, "fourier", "mesh"),
            P(None, None, "fourier", "mesh"),
            P(),
            P("mesh"),
            P("mesh", None),
            P("mesh", None),
        ),
        out_specs=P(None, None, "fourier", "mesh"),
        check_vma=False,
    )
```
